512 devices in a mesh: resp: 8 (over y_lo, core), tp: 16 (over y_hi, z), grp: 4 (over x).
Axes of the slice: x: 4, y: 8 (y_hi: 2, y_lo: 4; y = y_hi * 4 + y_lo), z: 8, core: 2. Of those that a mesh axis runs over, the one named last changes fastest.
Arguments:
- queries: bfloat16 [4096, 8192], P(('grp', 'resp'), 'tp'), parts along dimension 0, may hold values from -8 to 8
- resp_keys: bfloat16 [4096, 1024], P(('grp', 'resp')), parts along dimension 0, may hold values from -6 to 6
- resp_values: bfloat16 [4096, 1024], P(('grp', 'resp')), parts along dimension 0, may hold values from -6 to 6
- prefix_keys: bfloat16 [8192, 1024], P(('grp', 'resp', 'tp')), parts along dimension 0, may hold values from -8 to 8
- prefix_values: bfloat16 [8192, 1024], P(('grp', 'resp', 'tp')), parts along dimension 0, may hold values from -6 to 6
- cotangent: bfloat16 [4096, 8192], P(('grp', 'resp'), 'tp'), parts along dimension 0, may hold values from -96 to 96
- lengths: int32 [32], P('grp'), parts along dimension 0, may hold values from 1 to 128, 640 in all
Outputs:
- resp_dq: float32 [4096, 8192], P(('grp', 'resp'), 'tp'), parts along dimension 0
- resp_dk: float32 [4096, 1024], P(('grp', 'resp', 'tp')), parts along dimension 0
- resp_dv: float32 [4096, 1024], P(('grp', 'resp', 'tp')), parts along dimension 0
- prefix_dk: float32 [8192, 1024], P(('grp', 'tp'), 'resp'), parts along dimension 0
- prefix_dv: float32 [8192, 1024], P(('grp', 'tp'), 'resp'), parts along dimension 0
The draws below stay inside these ranges and needn't reach their ends.
There are 4 independent parts, one for each index of `grp`. The reference program is written for one: setup_inputs(seed, part) draws one part's arguments, and reference() takes and returns one part's arrays. A program takes and returns all parts, laid end to end along the dimension named above; each array names one. Nothing has to cross between parts.
All inputs are finite; a program needn't handle non-finite values.
Results may differ from the reference program's by a relative error of at most 0.0074.
Values may be sent and summed in bfloat16 or wider, within the bound.
A program may use at most 64 MiB of HBM per device.

```python
import math
import jax
import jax.numpy as jnp
import numpy as np
from jax import lax

QH = 64
KVH = 8
HD = 128
PREFIX = 2048
RESP_LEN = 128
RESP_ROWS = 1024
N_RESP = 8


def draw_queries(key, part):
    key = jax.random.fold_in(key, 11)
    base = jax.random.truncated_normal(key, -6.0, 6.0, (RESP_ROWS, QH * HD), jnp.float32)
    return base.astype(jnp.bfloat16)


def draw_prefix_keys(key, part):
    key = jax.random.fold_in(key, 23)
    base = jax.random.truncated_normal(key, -6.0, 6.0, (PREFIX, KVH * HD), jnp.float32)
    return base.astype(jnp.bfloat16)


def shard_levels(key, shape, cuts, low, top_value):
    factor_of = 1.0
    for axis_at, parts in cuts:
        draws = jax.random.uniform(jax.random.fold_in(jax.random.fold_in(key, 6), axis_at), (parts,), jnp.float32, low / len(cuts), top_value / len(cuts))
        factor_of = factor_of * jnp.repeat(jnp.exp(draws), shape[axis_at] // parts).reshape((-1,) + (1,) * (len(shape) - 1 - axis_at))
    return factor_of


def profile(amount, total, most, lean):
    portions = [(1 << 20) // math.isqrt(grade ** lean) + 1 for grade in range(2, amount + 1)]
    rest, given = total - most - (amount - 1), [1] * (amount - 1)
    while rest > 0:
        movable = [i for i in range(amount - 1) if given[i] < most]
        whole, budget = sum([portions[i] for i in movable]), rest
        for i in movable:
            extra = min(most - given[i], max(1, budget * portions[i] // whole), rest)
            given[i] = given[i] + extra
            rest = rest - extra
    return np.array([most] + given)


def uneven(rng, amount, total, most, skew):
    if amount == 2:
        one = jax.random.randint(rng, (), max(1, total - most), min(most, total - 1) + 1)
        return jnp.stack([one, total - one])
    sizes = jnp.asarray(profile(amount, total, most, skew), jnp.int32)
    twos = (amount - 1) // 2
    giver, receiver = sizes[1:1 + 2 * twos:2], sizes[2:2 + 2 * twos:2]
    room = jnp.minimum(giver - 1, most - receiver)
    passed = jax.random.randint(jax.random.fold_in(rng, 1), (twos,), 0, 1 << 20) % (room + 1)
    sizes = sizes.at[1:1 + 2 * twos:2].set(giver - passed).at[2:2 + 2 * twos:2].set(receiver + passed)
    return sizes[jax.random.permutation(jax.random.fold_in(rng, 2), amount)]


def noise(own_key, shape, scale, reach, cuts=(), dtype=jnp.bfloat16):
    gain = shard_levels(own_key, shape, cuts, -0.22, 0.18) if cuts else 1.0
    entries = jax.random.normal(own_key, shape, jnp.float32) * scale * gain
    return jnp.minimum(jnp.maximum(entries, -reach), reach).astype(dtype)


def setup_inputs(seed: int = 0, part: int = 0) -> dict:
    streams_of = jax.random.split(jax.random.key(seed), 8)
    part_keys = jax.random.split(jax.random.fold_in(streams_of[7], part), 8)
    return {
        "queries": draw_queries(jax.random.fold_in(jax.random.fold_in(streams_of[7], part), 71), part),
        "resp_keys": noise(part_keys[1], (RESP_ROWS, KVH * HD), 1.0, 6.0, ((0, 8),)),
        "resp_values": noise(part_keys[2], (RESP_ROWS, KVH * HD), 1.0, 6.0, ((0, 8),)),
        "prefix_keys": draw_prefix_keys(jax.random.fold_in(jax.random.fold_in(streams_of[7], part), 71), part),
        "prefix_values": noise(part_keys[4], (PREFIX, KVH * HD), 1.0, 6.0, ((0, 128),)),
        "cotangent": noise(part_keys[5], (RESP_ROWS, QH * HD), 16.0, 96.0, ((0, 8), (1, 16))),
        "lengths": uneven(part_keys[6], N_RESP, N_RESP * RESP_LEN * 5 // 8, RESP_LEN, 2).astype(jnp.int32),
    }


def attend(query, dout, keys, values):
    count = query.shape[1]
    total = keys.shape[0]
    prefix = total - count
    scale = 1.0 / math.sqrt(query.shape[2])
    query_f = query.astype(jnp.float32)
    keys_f = keys.astype(jnp.float32)
    values_f = values.astype(jnp.float32)
    dout_f = dout.astype(jnp.float32)
    scores = jnp.einsum('grd,sd->grs', query_f, keys_f) * scale
    row_pos = jnp.arange(count).astype(jnp.int32)[:, None]
    col_pos = jnp.arange(total).astype(jnp.int32)[None, :]
    allowed = (col_pos < prefix) | (col_pos - prefix <= row_pos)
    scores = jnp.where(allowed[None], scores, -jnp.inf)
    top = lax.optimization_barrier(jnp.max(scores, axis=-1, keepdims=True))
    expo = jnp.exp(scores - top)
    probs = expo / lax.optimization_barrier(jnp.sum(expo, axis=-1, keepdims=True))
    probs_b = lax.optimization_barrier(probs.astype(jnp.bfloat16)).astype(jnp.float32)
    attended = jnp.einsum('grs,sd->grd', probs_b, values_f)
    d_prob = jnp.einsum('grd,sd->grs', dout_f, values_f)
    delta = lax.optimization_barrier(jnp.sum(dout_f * attended, axis=-1, keepdims=True))
    d_score = lax.optimization_barrier((probs * (d_prob - delta)).astype(jnp.bfloat16)).astype(jnp.float32)
    grad_q = jnp.einsum('grs,sd->grd', d_score, keys_f) * scale
    grad_k = jnp.einsum('grs,grd->sd', d_score, query_f) * scale
    grad_v = jnp.einsum('grs,grd->sd', probs_b, dout_f)
    return (grad_q, grad_k, grad_v)

def reference(queries, resp_keys, resp_values, prefix_keys, prefix_values, cotangent, lengths):
    group = QH // KVH
    position = (jnp.arange(RESP_ROWS) % RESP_LEN).astype(jnp.int32)
    limit = jnp.repeat(lengths, RESP_LEN).astype(jnp.int32)
    masked = jnp.where((position < limit)[:, None], cotangent, jnp.zeros_like(cotangent))
    query_all = queries.reshape(N_RESP, RESP_LEN, KVH, group, HD).transpose(0, 2, 3, 1, 4)
    dout_all = masked.reshape(N_RESP, RESP_LEN, KVH, group, HD).transpose(0, 2, 3, 1, 4)
    own_keys = resp_keys.reshape(N_RESP, RESP_LEN, KVH, HD).transpose(0, 2, 1, 3)
    own_values = resp_values.reshape(N_RESP, RESP_LEN, KVH, HD).transpose(0, 2, 1, 3)
    shared_keys = prefix_keys.reshape(PREFIX, KVH, HD).transpose(1, 0, 2)
    shared_values = prefix_values.reshape(PREFIX, KVH, HD).transpose(1, 0, 2)

    def per_owner(owner_args):
        query, dout, keys, values = owner_args

        def per_head(head_args):
            head_q, head_d, head_k, head_v, pre_k, pre_v = head_args
            joined_k = jnp.concatenate([pre_k, head_k], 0)
            joined_v = jnp.concatenate([pre_v, head_v], 0)
            return attend(head_q, head_d, joined_k, joined_v)
        return lax.map(per_head, (query, dout, keys, values, shared_keys, shared_values))
    grad_q, grad_k, grad_v = lax.map(per_owner, (query_all, dout_all, own_keys, own_values))
    resp_dq = grad_q.transpose(0, 3, 1, 2, 4).reshape(RESP_ROWS, QH * HD)
    resp_dk = grad_k[:, :, PREFIX:].transpose(0, 2, 1, 3).reshape(RESP_ROWS, KVH * HD)
    resp_dv = grad_v[:, :, PREFIX:].transpose(0, 2, 1, 3).reshape(RESP_ROWS, KVH * HD)
    prefix_dk = lax.optimization_barrier(jnp.sum(grad_k[:, :, :PREFIX], axis=0)).transpose(1, 0, 2).reshape(PREFIX, KVH * HD)
    prefix_dv = lax.optimization_barrier(jnp.sum(grad_v[:, :, :PREFIX], axis=0)).transpose(1, 0, 2).reshape(PREFIX, KVH * HD)
    return (resp_dq, resp_dk, resp_dv, prefix_dk, prefix_dv)
```

```python
import functools
import math

import jax
import jax.numpy as jnp
from jax import lax
from jax.experimental import pallas as pl
from jax.experimental.pallas import tpu as pltpu
from jax.sharding import PartitionSpec as P

MESH = pl.DeviceIdType.MESH
HD = 128
CHUNK = 128
F32 = jnp.float32
BF16 = jnp.bfloat16


def flip(value, bits):
    if bits & 1:
        value = value + 1 - 2 * lax.rem(value, 2)
    if bits & 2:
        value = value + 2 - 4 * lax.rem(value // 2, 2)
    return value


def fold(x, op):
    return op(x.reshape(x.shape[0] // 8, 8, x.shape[1]), axis=0)


def kernel(
    n_resp,
    n_tp,
    q_hbm,
    rk_hbm,
    rv_hbm,
    pk_hbm,
    pv_hbm,
    ct_hbm,
    len_ref,
    dq_ref,
    rdk_ref,
    rdv_ref,
    pdk_ref,
    pdv_ref,
    pin,
    kv,
    rkv,
    q_s,
    do_s,
    q_t,
    do_t,
    st,
    dp,
    pb,
    st_r,
    dp_r,
    pb_r,
    mx,
    sm,
    dl,
    sib_send,
    sib_recv,
    acc,
    z_send,
    z_recv,
    y_send,
    y_recv,
    p_send,
    p_recv,
    rg_send,
    rg_recv,
    rg_acc,
    in_sem,
    a_send,
    a_recv,
    gy_send,
    gy_recv,
    gz_send,
    gz_recv,
    gs_send,
    gs_recv,
    fs_send,
    fs_recv,
    fz_send,
    fz_recv,
    fy_send,
    fy_recv,
    fp_send,
    fp_recv,
    rg_ssem,
    rg_rsem,
):
    r = lax.axis_index("resp")
    t = lax.axis_index("tp")
    n_y = n_resp // 2
    y, c = r // 2, lax.rem(r, 2)
    g, h = t // 2, lax.rem(t, 2)
    count = q_hbm.shape[0]
    heads = q_hbm.shape[1] // HD
    scale = 1.0 / math.sqrt(HD)
    block = kv.shape[2]
    half = block // 2

    sibling = {"resp": flip(r, 1), "tp": t}
    zpair = {"resp": r, "tp": flip(t, 1)}

    def yline(k):
        return {"resp": 2 * flip(y, k) + c, "tp": t}

    owner = {"resp": g, "tp": 2 * r + h}
    away = jnp.logical_not(r == g)

    def rcopy(src, dst, send, recv, dev):
        return pltpu.make_async_remote_copy(
            src_ref=src, dst_ref=dst, send_sem=send, recv_sem=recv, device_id=dev, device_id_type=MESH
        )

    col = pl.multiple_of(g * HD, HD)
    loads = [
        pltpu.make_async_copy(pk_hbm, pin.at[0], in_sem.at[0]),
        pltpu.make_async_copy(pv_hbm, pin.at[1], in_sem.at[1]),
        pltpu.make_async_copy(rk_hbm.at[:, pl.ds(col, HD)], rkv.at[0], in_sem.at[2]),
        pltpu.make_async_copy(rv_hbm.at[:, pl.ds(col, HD)], rkv.at[1], in_sem.at[3]),
    ]
    for j in range(heads):
        rows = pl.ds(j * count, count)
        loads.append(pltpu.make_async_copy(q_hbm.at[:, pl.ds(j * HD, HD)], q_s.at[rows], in_sem.at[4 + j]))
        loads.append(
            pltpu.make_async_copy(ct_hbm.at[:, pl.ds(j * HD, HD)], do_s.at[rows], in_sem.at[4 + heads + j])
        )
    for load in loads:
        load.start()

    barrier = pltpu.get_barrier_semaphore()

    def greet(d, carry):
        pl.semaphore_signal(
            barrier, inc=1, device_id={"resp": r, "tp": lax.rem(t + d, n_tp)}, device_id_type=MESH
        )
        return carry

    lax.fori_loop(1, n_tp, greet, 0)
    pl.semaphore_signal(barrier, inc=1, device_id=sibling, device_id_type=MESH)
    for k in range(1, n_y):
        pl.semaphore_signal(barrier, inc=1, device_id=yline(k), device_id_type=MESH)

    @pl.when(away)
    def _():
        pl.semaphore_signal(barrier, inc=1, device_id=owner, device_id_type=MESH)

    pl.semaphore_wait(barrier, n_tp - 1 + n_y + away.astype(jnp.int32))

    rows16 = pl.ds(pl.multiple_of(t * 16, 16), 16)
    for a in range(2):
        loads[a].wait()

        def scatter(d, carry, a=a):
            to = lax.rem(t + d, n_tp)
            rcopy(
                pin.at[a, :, pl.ds(pl.multiple_of((to // 2) * HD, HD), HD)],
                kv.at[a, r, rows16],
                a_send.at[a],
                a_recv.at[a],
                {"resp": r, "tp": to},
            ).start()
            return carry

        lax.fori_loop(1, n_tp, scatter, 0)
        pltpu.make_async_copy(pin.at[a, :, pl.ds(col, HD)], kv.at[a, r, rows16], a_recv.at[a]).start()

    for load in loads[2:]:
        load.wait()
    q_t[...] = jnp.transpose(q_s[...].astype(F32)).astype(BF16)
    length = len_ref[r]
    live = lax.rem(lax.broadcasted_iota(jnp.int32, do_s.shape, 0), count) < length
    masked = jnp.where(live, do_s[...].astype(F32), 0.0)
    do_s[...] = masked.astype(BF16)
    do_t[...] = jnp.transpose(masked).astype(BF16)

    s = jnp.dot(rkv[0], q_t[...], preferred_element_type=F32) * scale
    key_pos = lax.broadcasted_iota(jnp.int32, s.shape, 0)
    row_pos = lax.rem(lax.broadcasted_iota(jnp.int32, s.shape, 1), count)
    s = jnp.where(key_pos <= row_pos, s, -jnp.inf)
    st_r[...] = s
    mx[...] = fold(s, jnp.max)

    def mine(k):
        return 2 * flip(y, k) + c

    def other(k):
        return 2 * flip(y, k) + 1 - c

    own_half = pl.ds(pl.multiple_of(h * half, half), half)
    far_half = pl.ds(pl.multiple_of((1 - h) * half, half), half)

    sends = []

    def start(copy):
        copy.start()
        sends.append(copy)

    def gather_first(a):
        pltpu.make_async_copy(kv.at[a, r], kv.at[a, r], a_recv.at[a]).wait()
        for k in range(n_y - 1, 0, -1):
            ref = kv.at[a, r, own_half]
            start(rcopy(ref, ref, gy_send.at[a, k], gy_recv.at[a, k], yline(k)))
        start(rcopy(kv.at[a, r], kv.at[a, r], gs_send.at[a, 0, 0], gs_recv.at[a, 0, 0], sibling))

    def gather_y(a, k):
        ref = kv.at[a, mine(k), own_half]
        rcopy(ref, ref, gy_send.at[a, k], gy_recv.at[a, k], yline(k)).wait_recv()
        start(rcopy(ref, ref, gz_send.at[a, k], gz_recv.at[a, k], zpair))
        start(rcopy(ref, ref, gs_send.at[a, k, 0], gs_recv.at[a, k, 0], sibling))

    def gather_z(a, k):
        ref = kv.at[a, mine(k), far_half]
        rcopy(ref, ref, gz_send.at[a, k], gz_recv.at[a, k], zpair).wait_recv()
        start(rcopy(ref, ref, gs_send.at[a, k, 1], gs_recv.at[a, k, 1], sibling))

    def gather_sib(a, k):
        if k == 0:
            ref = kv.at[a, other(0)]
            rcopy(ref, ref, gs_send.at[a, 0, 0], gs_recv.at[a, 0, 0], sibling).wait_recv()
            return
        for i, part in enumerate((own_half, far_half)):
            ref = kv.at[a, other(k), part]
            rcopy(ref, ref, gs_send.at[a, k, i], gs_recv.at[a, k, i], sibling).wait_recv()

    n_sub = block // CHUNK

    def over(fn, blocks):
        for b in blocks:

            def sub(i, carry, b=b):
                fn(b, pl.ds(pl.multiple_of(i * CHUNK, CHUNK), CHUNK))
                return carry

            lax.fori_loop(0, n_sub, sub, 0)

    def over_all(fn):
        def one(i, carry):
            fn(i // n_sub, pl.ds(pl.multiple_of(lax.rem(i, n_sub) * CHUNK, CHUNK), CHUNK))
            return carry

        lax.fori_loop(0, n_resp * n_sub, one, 0)

    def score(b, rows):
        s = jnp.dot(kv[0, b, rows], q_t[...], preferred_element_type=F32) * scale
        st[b, rows] = s
        mx[...] = jnp.maximum(mx[...], fold(s, jnp.max))

    order = [k for k in (1, 3, 2) if k < n_y]
    gather_first(0)
    gather_first(1)
    over(score, [r])
    gather_sib(0, 0)
    over(score, [other(0)])
    for k in order:
        gather_y(0, k)
    for k in order:
        gather_z(0, k)
        over(score, [mine(k)])
    for k in order:
        gather_y(1, k)
    for k in order:
        gather_sib(0, k)
        over(score, [other(k)])

    mx[...] = jnp.broadcast_to(jnp.max(mx[...], axis=0, keepdims=True), mx.shape)
    m3 = mx[...][None]

    def expo(x):
        x3 = x.reshape(x.shape[0] // 8, 8, x.shape[1])
        return jnp.exp(x3 - mx[...][None]).reshape(x.shape)

    def times(x, v):
        return (x.reshape(x.shape[0] // 8, 8, x.shape[1]) * v[None]).reshape(x.shape)

    def minus(x, v):
        return (x.reshape(x.shape[0] // 8, 8, x.shape[1]) - v[None]).reshape(x.shape)

    e = expo(st_r[...])
    st_r[...] = e
    sm[...] = fold(e, jnp.sum)

    def soften(b, rows):
        e = expo(st[b, rows])
        st[b, rows] = e
        sm[...] += fold(e, jnp.sum)

    over_all(soften)
    sm[...] = jnp.broadcast_to(1.0 / jnp.sum(sm[...], axis=0, keepdims=True), sm.shape)
    for k in order:
        gather_z(1, k)

    def grad_out(a, b, rows, keep, value, yy):
        sel = rows.start // half
        if keep:
            acc[a, yy, sel] = value
        else:
            sib_send[a, yy, sel] = value.astype(BF16)

    def dv_chunk(yy, rows, keep):
        b = 2 * yy + (c if keep else 1 - c)
        p = times(st[b, rows], sm[...]).astype(BF16)
        pb[b, rows] = p
        grad_out(1, b, rows, keep, jnp.dot(p, do_s[...], preferred_element_type=F32), yy)

    def dk_chunk(yy, rows, keep):
        b = 2 * yy + (c if keep else 1 - c)
        ds = (times(st[b, rows], sm[...]) * minus(dp[b, rows], dl[...])).astype(BF16)
        pb[b, rows] = ds
        grad_out(0, b, rows, keep, jnp.dot(ds, q_s[...], preferred_element_type=F32) * scale, yy)

    def grad_pass(a, fn):
        for k in range(n_y - 1, -1, -1):
            yy = flip(y, k)
            over(lambda v, rows: fn(v, rows, False), [yy])
            start(
                rcopy(
                    sib_send.at[a, yy], sib_recv.at[a, yy], fs_send.at[a, k], fs_recv.at[a, k], sibling
                )
            )
        for k in range(n_y - 1, -1, -1):
            over(lambda v, rows: fn(v, rows, True), [flip(y, k)])

    def sum_sib(a):
        for k in range(n_y - 1, -1, -1):
            yy = flip(y, k)
            rcopy(
                sib_send.at[a, yy], sib_recv.at[a, yy], fs_send.at[a, k], fs_recv.at[a, k], sibling
            ).wait_recv()
            z_send[a, k] = (acc[a, yy, 1 - h] + sib_recv[a, yy, 1 - h].astype(F32)).astype(BF16)
            start(rcopy(z_send.at[a, k], z_recv.at[a, k], fz_send.at[a, k], fz_recv.at[a, k], zpair))
            acc[a, yy, h] += sib_recv[a, yy, h].astype(F32)

    def sum_z(a):
        for k in range(n_y - 1, -1, -1):
            yy = flip(y, k)
            rcopy(z_send.at[a, k], z_recv.at[a, k], fz_send.at[a, k], fz_recv.at[a, k], zpair).wait_recv()
            total = acc[a, yy, h] + z_recv[a, k].astype(F32)
            if k:
                y_send[a, k] = total.astype(BF16)
                start(rcopy(y_send.at[a, k], y_recv.at[a, k], fy_send.at[a, k], fy_recv.at[a, k], yline(k)))
            else:
                acc[a, yy, h] = total

    def sum_y(a):
        total = acc[a, y, h]
        for k in order:
            rcopy(y_send.at[a, k], y_recv.at[a, k], fy_send.at[a, k], fy_recv.at[a, k], yline(k)).wait_recv()
            total = total + y_recv[a, k].astype(F32)
        p_send[a] = total.astype(BF16)
        home = rcopy(p_send.at[a], p_recv.at[a], fp_send.at[a], fp_recv.at[a], owner)
        local = pltpu.make_async_copy(p_send.at[a], p_recv.at[a], fp_recv.at[a])

        @pl.when(away)
        def _():
            home.start()

        @pl.when(r == g)
        def _():
            local.start()

        return home

    p = times(st_r[...], sm[...]).astype(BF16)
    pb_r[...] = p
    rg_acc[1] = jnp.dot(p, do_s[...], preferred_element_type=F32)
    grad_pass(1, dv_chunk)
    sum_sib(1)

    d = jnp.dot(rkv[1], do_t[...], preferred_element_type=F32)
    dp_r[...] = d
    dl[...] = fold(pb_r[...].astype(F32) * d, jnp.sum)

    def dprob(b, rows):
        d = jnp.dot(kv[1, b, rows], do_t[...], preferred_element_type=F32)
        dp[b, rows] = d
        dl[...] += fold(pb[b, rows].astype(F32) * d, jnp.sum)

    over(dprob, [r])
    gather_sib(1, 0)
    over(dprob, [other(0)])
    for k in order:
        over(dprob, [mine(k)])
    for k in order:
        gather_sib(1, k)
        over(dprob, [other(k)])
    dl[...] = jnp.broadcast_to(jnp.sum(dl[...], axis=0, keepdims=True), dl.shape)
    sum_z(1)

    ds = (times(st_r[...], sm[...]) * minus(dp_r[...], dl[...])).astype(BF16)
    pb_r[...] = ds
    rg_acc[0] = jnp.dot(ds, q_s[...], preferred_element_type=F32) * scale
    own_rows = count // n_tp
    rg = jnp.concatenate(
        [rg_acc[0].reshape(n_tp, own_rows, HD), rg_acc[1].reshape(n_tp, own_rows, HD)], axis=1
    )
    rg_send[...] = rg.astype(BF16)

    def spread(d, carry):
        to = lax.rem(t + d, n_tp)
        rcopy(rg_send.at[to], rg_recv.at[t], rg_ssem.at[0], rg_rsem.at[0], {"resp": r, "tp": to}).start()
        return carry

    lax.fori_loop(1, n_tp, spread, 0)
    pltpu.make_async_copy(rg_send.at[t], rg_recv.at[t], rg_rsem.at[0]).start()

    grad_pass(0, dk_chunk)
    sum_sib(0)
    home_v = sum_y(1)

    def tdot(a, b):
        return lax.dot_general(a, b, (((0,), (0,)), ((), ())), preferred_element_type=F32)

    sum_z(0)

    def dq_block(b, total):
        return total + tdot(kv[0, b], pb[b])

    dq_t = lax.fori_loop(0, n_resp, dq_block, tdot(rkv[0], pb_r[...]))
    for j in range(heads):
        dq_ref[:, j * HD : (j + 1) * HD] = jnp.transpose(dq_t[:, j * count : (j + 1) * count]) * scale
    home_k = sum_y(0)

    pltpu.make_async_copy(rg_recv, rg_recv, rg_rsem.at[0]).wait()
    got = rg_recv[...].astype(F32)
    for i in range(n_tp // 2):
        both = got[2 * i] + got[2 * i + 1]
        rdk_ref[:, i * HD : (i + 1) * HD] = both[:own_rows]
        rdv_ref[:, i * HD : (i + 1) * HD] = both[own_rows:]

    home_v.wait_recv()
    pdv_ref[...] = p_recv[1].astype(F32)
    home_k.wait_recv()
    pdk_ref[...] = p_recv[0].astype(F32)

    for a in range(2):
        pltpu.make_async_copy(
            kv.at[a, 0, pl.ds(0, (n_tp - 1) * 16)], kv.at[a, 0, pl.ds(0, (n_tp - 1) * 16)], a_send.at[a]
        ).wait()
    pltpu.make_async_copy(
        rg_send.at[pl.ds(0, n_tp - 1)], rg_send.at[pl.ds(0, n_tp - 1)], rg_ssem.at[0]
    ).wait()
    for copy in sends:
        copy.wait_send()

    @pl.when(away)
    def _():
        home_v.wait_send()
        home_k.wait_send()


def solution(mesh):
    n_resp, n_tp = mesh.shape["resp"], mesh.shape["tp"]
    n_y = n_resp // 2

    def per_device(queries, resp_keys, resp_values, prefix_keys, prefix_values, cotangent, lengths):
        count, width = queries.shape
        heads = width // HD
        rows = heads * count
        block = n_tp * prefix_keys.shape[0]
        half = block // 2
        cols = prefix_keys.shape[1]
        dma = pltpu.SemaphoreType.DMA
        vmem = pltpu.VMEM
        any_spec = pl.BlockSpec(memory_space=pl.ANY)
        vmem_spec = pl.BlockSpec(memory_space=pltpu.VMEM)
        return pl.pallas_call(
            functools.partial(kernel, n_resp, n_tp),
            out_shape=(
                jax.ShapeDtypeStruct((count, width), F32),
                jax.ShapeDtypeStruct((count // n_tp, cols), F32),
                jax.ShapeDtypeStruct((count // n_tp, cols), F32),
                jax.ShapeDtypeStruct((half, HD), F32),
                jax.ShapeDtypeStruct((half, HD), F32),
            ),
            in_specs=[any_spec] * 6 + [pl.BlockSpec(memory_space=pltpu.SMEM)],
            out_specs=(vmem_spec,) * 5,
            scratch_shapes=[
                vmem((2, 16, cols), BF16),
                vmem((2, n_resp, block, HD), BF16),
                vmem((2, count, HD), BF16),
                vmem((rows, HD), BF16),
                vmem((rows, HD), BF16),
                vmem((HD, rows), BF16),
                vmem((HD, rows), BF16),
                vmem((n_resp, block, rows), F32),
                vmem((n_resp, block, rows), F32),
                vmem((n_resp, block, rows), BF16),
                vmem((count, rows), F32),
                vmem((count, rows), F32),
                vmem((count, rows), BF16),
                vmem((8, rows), F32),
                vmem((8, rows), F32),
                vmem((8, rows), F32),
                vmem((2, n_y, 2, half, HD), BF16),
                vmem((2, n_y, 2, half, HD), BF16),
                vmem((2, n_y, 2, half, HD), F32),
                vmem((2, n_y, half, HD), BF16),
                vmem((2, n_y, half, HD), BF16),
                vmem((2, n_y, half, HD), BF16),
                vmem((2, n_y, half, HD), BF16),
                vmem((2, half, HD), BF16),
                vmem((2, half, HD), BF16),
                vmem((n_tp, 16, HD), BF16),
                vmem((n_tp, 16, HD), BF16),
                vmem((2, count, HD), F32),
                dma((4 + 2 * heads,)),
                dma((2,)),
                dma((2,)),
                dma((2, n_y)),
                dma((2, n_y)),
                dma((2, n_y)),
                dma((2, n_y)),
                dma((2, n_y, 2)),
                dma((2, n_y, 2)),
                dma((2, n_y)),
                dma((2, n_y)),
                dma((2, n_y)),
                dma((2, n_y)),
                dma((2, n_y)),
                dma((2, n_y)),
                dma((2,)),
                dma((2,)),
                dma((1,)),
                dma((1,)),
            ],
            compiler_params=pltpu.CompilerParams(
                collective_id=0, has_side_effects=True, vmem_limit_bytes=48 * 1024 * 1024
            ),
            cost_estimate=pl.CostEstimate(
                flops=10 * rows * (n_resp * block + count) * HD,
                bytes_accessed=4 * 1024 * 1024,
                transcendentals=rows * (n_resp * block + count),
            ),
        )(queries, resp_keys, resp_values, prefix_keys, prefix_values, cotangent, lengths)

    return jax.shard_map(
        per_device,
        mesh=mesh,
        in_specs=(
            P(("grp", "resp"), "tp"),
            P(("grp", "resp"), None),
            P(("grp", "resp"), None),
            P(("grp", "resp", "tp"), None),
            P(("grp", "resp", "tp"), None),
            P(("grp", "resp"), "tp"),
            P("grp"),
        ),
        out_specs=(
            P(("grp", "resp"), "tp"),
            P(("grp", "resp", "tp"), None),
            P(("grp", "resp", "tp"), None),
            P(("grp", "tp"), "resp"),
            P(("grp", "tp"), "resp"),
        ),
        check_vma=False,
    )
```

```python
import functools
import math

import jax
import jax.numpy as jnp
from jax import lax
from jax.experimental import pallas as pl
from jax.experimental.pallas import tpu as pltpu
from jax.sharding import PartitionSpec as P

MESH = pl.DeviceIdType.MESH
HD = 128
CHUNK = 128
F32 = jnp.float32
BF16 = jnp.bfloat16


def flip(value, bits):
    if bits & 1:
        value = value + 1 - 2 * lax.rem(value, 2)
    if bits & 2:
        value = value + 2 - 4 * lax.rem(value // 2, 2)
    return value


def fold(x, op):
    return op(x.reshape(x.shape[0] // 8, 8, x.shape[1]), axis=0)


def kernel(
    n_resp,
    n_tp,
    q_hbm,
    rk_hbm,
    rv_hbm,
    pk_hbm,
    pv_hbm,
    ct_hbm,
    len_ref,
    dq_ref,
    rdk_ref,
    rdv_ref,
    pdk_ref,
    pdv_ref,
    pin,
    kv,
    rkv,
    q_s,
    do_s,
    q_t,
    do_t,
    st,
    dp,
    pb,
    st_r,
    dp_r,
    pb_r,
    mx,
    sm,
    dl,
    sib_send,
    sib_recv,
    acc,
    z_send,
    z_recv,
    y_send,
    y_recv,
    p_send,
    p_recv,
    rg_send,
    rg_recv,
    rg_acc,
    sent,
    in_sem,
    a_send,
    a_recv,
    gs_send,
    gs_recv,
    fs_send,
    fs_recv,
    fz_send,
    fz_recv,
    fy_send,
    fy_recv,
    fp_send,
    fp_recv,
    rg_ssem,
    rg_rsem,
):
    r = lax.axis_index("resp")
    t = lax.axis_index("tp")
    n_y = n_resp // 2
    y, c = r // 2, lax.rem(r, 2)
    g, h = t // 2, lax.rem(t, 2)
    count = q_hbm.shape[0]
    heads = q_hbm.shape[1] // HD
    scale = 1.0 / math.sqrt(HD)
    block = kv.shape[2]
    half = block // 2

    sibling = {"resp": flip(r, 1), "tp": t}
    zpair = {"resp": r, "tp": flip(t, 1)}

    def yline(k):
        return {"resp": 2 * flip(y, k) + c, "tp": t}

    owner = {"resp": g, "tp": 2 * r + h}
    away = jnp.logical_not(r == g)

    def rcopy(src, dst, send, recv, dev):
        return pltpu.make_async_remote_copy(
            src_ref=src, dst_ref=dst, send_sem=send, recv_sem=recv, device_id=dev, device_id_type=MESH
        )

    col = pl.multiple_of(g * HD, HD)
    loads = [
        pltpu.make_async_copy(pk_hbm, pin.at[0], in_sem.at[0]),
        pltpu.make_async_copy(pv_hbm, pin.at[1], in_sem.at[1]),
        pltpu.make_async_copy(rk_hbm.at[:, pl.ds(col, HD)], rkv.at[0], in_sem.at[2]),
        pltpu.make_async_copy(rv_hbm.at[:, pl.ds(col, HD)], rkv.at[1], in_sem.at[3]),
    ]
    for j in range(heads):
        rows = pl.ds(j * count, count)
        loads.append(pltpu.make_async_copy(q_hbm.at[:, pl.ds(j * HD, HD)], q_s.at[rows], in_sem.at[4 + j]))
        loads.append(
            pltpu.make_async_copy(ct_hbm.at[:, pl.ds(j * HD, HD)], do_s.at[rows], in_sem.at[4 + heads + j])
        )
    for load in loads:
        load.start()

    n_z = n_tp // 2
    n_ring = 2 * n_y
    y_all, z = lax.rem(t, n_tp) // n_z * n_y + y, lax.rem(t, n_z)
    ys = [lax.rem(y_all + d, n_ring) for d in range(n_ring)]
    zs = [lax.rem(z + d, n_z) for d in range(n_z)]
    resp_of = [2 * lax.rem(v, n_y) + c for v in ys]
    tp_of = [v // n_y * n_z for v in ys]

    def hops(d, n):
        return min(d, n - d)

    offsets = [(i, j) for i in range(n_ring) for j in range(n_z) if i or j]
    offsets.sort(key=lambda o: -hops(o[0], n_ring) - hops(o[1], n_z))

    barrier = pltpu.get_barrier_semaphore()
    for i, j in offsets:
        pl.semaphore_signal(
            barrier, inc=1, device_id={"resp": resp_of[i], "tp": tp_of[i] + zs[j]}, device_id_type=MESH
        )
    pl.semaphore_signal(barrier, inc=1, device_id=sibling, device_id_type=MESH)

    @pl.when(away)
    def _():
        pl.semaphore_signal(barrier, inc=1, device_id=owner, device_id_type=MESH)

    for a in range(2):
        loads[a].wait()
    pl.semaphore_wait(barrier, len(offsets) + 1 + away.astype(jnp.int32))

    rows16 = pl.ds(pl.multiple_of(t * 16, 16), 16)
    spot = c * n_y + y
    for a in range(2):
        for i, j in offsets:
            to = tp_of[i] + zs[j]
            rcopy(
                pin.at[a, :, pl.ds(pl.multiple_of(to // 2 * HD, HD), HD)],
                kv.at[a, spot, rows16],
                a_send.at[a],
                a_recv.at[a],
                {"resp": resp_of[i], "tp": to},
            ).start()
        pltpu.make_async_copy(pin.at[a, :, pl.ds(col, HD)], kv.at[a, spot, rows16], a_recv.at[a]).start()

    for load in loads[2:]:
        load.wait()
    q_t[...] = jnp.transpose(q_s[...].astype(F32)).astype(BF16)
    length = len_ref[r]
    live = lax.rem(lax.broadcasted_iota(jnp.int32, do_s.shape, 0), count) < length
    masked = jnp.where(live, do_s[...].astype(F32), 0.0)
    do_s[...] = masked.astype(BF16)
    do_t[...] = jnp.transpose(masked).astype(BF16)

    s = jnp.dot(rkv[0], q_t[...], preferred_element_type=F32) * scale
    key_pos = lax.broadcasted_iota(jnp.int32, s.shape, 0)
    row_pos = lax.rem(lax.broadcasted_iota(jnp.int32, s.shape, 1), count)
    s = jnp.where(key_pos <= row_pos, s, -jnp.inf)
    st_r[...] = s
    mx[...] = fold(s, jnp.max)

    sends = []

    def start(copy):
        copy.start()
        sends.append(copy)

    near = pl.ds(c * n_y, n_y)
    far = pl.ds((1 - c) * n_y, n_y)

    def gather(a):
        pltpu.make_async_copy(kv.at[a, near], kv.at[a, near], a_recv.at[a]).wait()
        start(rcopy(kv.at[a, near], kv.at[a, near], gs_send.at[a], gs_recv.at[a], sibling))

    def gather_sib(a):
        rcopy(kv.at[a, far], kv.at[a, far], gs_send.at[a], gs_recv.at[a], sibling).wait_recv()

    n_sub = block // CHUNK

    def over(fn, first, blocks):
        def one(i, carry):
            fn(first + i // n_sub, pl.ds(pl.multiple_of(lax.rem(i, n_sub) * CHUNK, CHUNK), CHUNK))
            return carry

        lax.fori_loop(0, blocks * n_sub, one, 0)

    def score(b, rows):
        s = jnp.dot(kv[0, b, rows], q_t[...], preferred_element_type=F32) * scale
        st[b, rows] = s
        mx[...] = jnp.maximum(mx[...], fold(s, jnp.max))

    order = [k for k in (1, 3, 2) if k < n_y]
    gather(0)
    over(score, c * n_y, n_y)
    gather_sib(0)
    over(score, (1 - c) * n_y, n_y)

    mx[...] = jnp.broadcast_to(jnp.max(mx[...], axis=0, keepdims=True), mx.shape)
    m3 = mx[...][None]

    def expo(x):
        x3 = x.reshape(x.shape[0] // 8, 8, x.shape[1])
        return jnp.exp(x3 - mx[...][None]).reshape(x.shape)

    def times(x, v):
        return (x.reshape(x.shape[0] // 8, 8, x.shape[1]) * v[None]).reshape(x.shape)

    def minus(x, v):
        return (x.reshape(x.shape[0] // 8, 8, x.shape[1]) - v[None]).reshape(x.shape)

    e = expo(st_r[...])
    st_r[...] = e
    sm[...] = fold(e, jnp.sum)

    def soften(b, rows):
        e = expo(st[b, rows])
        st[b, rows] = e
        sm[...] += fold(e, jnp.sum)

    over(soften, 0, n_resp)
    sm[...] = jnp.broadcast_to(1.0 / jnp.sum(sm[...], axis=0, keepdims=True), sm.shape)

    def grad_out(a, b, rows, keep, value, yy):
        sel = rows.start // half
        if keep:
            acc[a, yy, sel] = value
        else:
            sib_send[a, yy, sel] = value.astype(BF16)

    def dv_chunk(b, rows, keep):
        p = times(st[b, rows], sm[...]).astype(BF16)
        pb[b, rows] = p
        grad_out(1, b, rows, keep, jnp.dot(p, do_s[...], preferred_element_type=F32), lax.rem(b, n_y))

    def dk_chunk(b, rows, keep):
        ds = (times(st[b, rows], sm[...]) * minus(dp[b, rows], dl[...])).astype(BF16)
        pb[b, rows] = ds
        grad_out(0, b, rows, keep, jnp.dot(ds, q_s[...], preferred_element_type=F32) * scale, lax.rem(b, n_y))

    def grad_pass(a, fn):
        for k in range(n_y - 1, -1, -1):
            yy = flip(y, k)
            over(lambda b, rows: fn(b, rows, False), (1 - c) * n_y + yy, 1)
            start(
                rcopy(
                    sib_send.at[a, yy], sib_recv.at[a, yy], fs_send.at[a, k], fs_recv.at[a, k], sibling
                )
            )
        for k in range(n_y - 1, -1, -1):
            yy = flip(y, k)
            over(lambda b, rows: fn(b, rows, True), c * n_y + yy, 1)
            rcopy(
                sib_send.at[a, yy], sib_recv.at[a, yy], fs_send.at[a, k], fs_recv.at[a, k], sibling
            ).wait_recv()
            z_send[a, k] = (acc[a, yy, 1 - h] + sib_recv[a, yy, 1 - h].astype(F32)).astype(BF16)
            start(rcopy(z_send.at[a, k], z_recv.at[a, k], fz_send.at[a, k], fz_recv.at[a, k], zpair))
            acc[a, yy, h] += sib_recv[a, yy, h].astype(F32)

    def sum_z(a):
        for k in range(n_y - 1, -1, -1):
            yy = flip(y, k)
            rcopy(z_send.at[a, k], z_recv.at[a, k], fz_send.at[a, k], fz_recv.at[a, k], zpair).wait_recv()
            total = acc[a, yy, h] + z_recv[a, k].astype(F32)
            if k:
                y_send[a, k] = total.astype(BF16)
                start(rcopy(y_send.at[a, k], y_recv.at[a, k], fy_send.at[a, k], fy_recv.at[a, k], yline(k)))
            else:
                acc[a, yy, h] = total

    def sum_y(a):
        total = acc[a, y, h]
        for k in order:
            rcopy(y_send.at[a, k], y_recv.at[a, k], fy_send.at[a, k], fy_recv.at[a, k], yline(k)).wait_recv()
            total = total + y_recv[a, k].astype(F32)
        p_send[a] = total.astype(BF16)
        home = rcopy(p_send.at[a], p_recv.at[a], fp_send.at[a], fp_recv.at[a], owner)
        local = pltpu.make_async_copy(p_send.at[a], p_recv.at[a], fp_recv.at[a])

        @pl.when(away)
        def _():
            home.start()

        @pl.when(r == g)
        def _():
            local.start()

        return home

    p = times(st_r[...], sm[...]).astype(BF16)
    pb_r[...] = p
    rg_acc[1] = jnp.dot(p, do_s[...], preferred_element_type=F32)
    grad_pass(1, dv_chunk)
    gather(1)

    d = jnp.dot(rkv[1], do_t[...], preferred_element_type=F32)
    dp_r[...] = d
    dl[...] = fold(pb_r[...].astype(F32) * d, jnp.sum)

    def dprob(b, rows):
        d = jnp.dot(kv[1, b, rows], do_t[...], preferred_element_type=F32)
        dp[b, rows] = d
        dl[...] += fold(pb[b, rows].astype(F32) * d, jnp.sum)

    over(dprob, c * n_y, n_y)
    sum_z(1)
    gather_sib(1)
    over(dprob, (1 - c) * n_y, n_y)
    dl[...] = jnp.broadcast_to(jnp.sum(dl[...], axis=0, keepdims=True), dl.shape)

    ds = (times(st_r[...], sm[...]) * minus(dp_r[...], dl[...])).astype(BF16)
    pb_r[...] = ds
    rg_acc[0] = jnp.dot(ds, q_s[...], preferred_element_type=F32) * scale
    own_rows = count // n_tp
    rg = jnp.concatenate(
        [rg_acc[0].reshape(n_tp, own_rows, HD), rg_acc[1].reshape(n_tp, own_rows, HD)], axis=1
    )
    rg_send[...] = rg.astype(BF16)

    def spread(d, carry):
        to = lax.rem(t + d, n_tp)
        rcopy(rg_send.at[to], rg_recv.at[t], rg_ssem.at[0], rg_rsem.at[0], {"resp": r, "tp": to}).start()
        return carry

    lax.fori_loop(1, n_tp, spread, 0)
    pltpu.make_async_copy(rg_send.at[t], rg_recv.at[t], rg_rsem.at[0]).start()

    grad_pass(0, dk_chunk)
    home_v = sum_y(1)

    def tdot(a, b):
        return lax.dot_general(a, b, (((0,), (0,)), ((), ())), preferred_element_type=F32)

    def dq_block(b, total):
        return total + tdot(kv[0, b], pb[b])

    dq_t = lax.fori_loop(0, n_resp, dq_block, tdot(rkv[0], pb_r[...]))
    for j in range(heads):
        dq_ref[:, j * HD : (j + 1) * HD] = jnp.transpose(dq_t[:, j * count : (j + 1) * count]) * scale
    sum_z(0)

    pltpu.make_async_copy(rg_recv, rg_recv, rg_rsem.at[0]).wait()
    got = rg_recv[...].astype(F32)
    for i in range(n_tp // 2):
        both = got[2 * i] + got[2 * i + 1]
        rdk_ref[:, i * HD : (i + 1) * HD] = both[:own_rows]
        rdv_ref[:, i * HD : (i + 1) * HD] = both[own_rows:]

    home_k = sum_y(0)
    home_v.wait_recv()
    pdv_ref[...] = p_recv[1].astype(F32)
    home_k.wait_recv()
    pdk_ref[...] = p_recv[0].astype(F32)

    for a in range(2):
        pltpu.make_async_copy(
            sent.at[pl.ds(0, len(offsets))], sent.at[pl.ds(0, len(offsets))], a_send.at[a]
        ).wait()
    pltpu.make_async_copy(
        rg_send.at[pl.ds(0, n_tp - 1)], rg_send.at[pl.ds(0, n_tp - 1)], rg_ssem.at[0]
    ).wait()
    for copy in sends:
        copy.wait_send()

    @pl.when(away)
    def _():
        home_v.wait_send()
        home_k.wait_send()


def solution(mesh):
    n_resp, n_tp = mesh.shape["resp"], mesh.shape["tp"]
    n_y = n_resp // 2

    def per_device(queries, resp_keys, resp_values, prefix_keys, prefix_values, cotangent, lengths):
        count, width = queries.shape
        heads = width // HD
        rows = heads * count
        block = n_tp * prefix_keys.shape[0]
        half = block // 2
        cols = prefix_keys.shape[1]
        dma = pltpu.SemaphoreType.DMA
        vmem = pltpu.VMEM
        any_spec = pl.BlockSpec(memory_space=pl.ANY)
        vmem_spec = pl.BlockSpec(memory_space=pltpu.VMEM)
        return pl.pallas_call(
            functools.partial(kernel, n_resp, n_tp),
            out_shape=(
                jax.ShapeDtypeStruct((count, width), F32),
                jax.ShapeDtypeStruct((count // n_tp, cols), F32),
                jax.ShapeDtypeStruct((count // n_tp, cols), F32),
                jax.ShapeDtypeStruct((half, HD), F32),
                jax.ShapeDtypeStruct((half, HD), F32),
            ),
            in_specs=[any_spec] * 6 + [pl.BlockSpec(memory_space=pltpu.SMEM)],
            out_specs=(vmem_spec,) * 5,
            scratch_shapes=[
                vmem((2, 16, cols), BF16),
                vmem((2, n_resp, block, HD), BF16),
                vmem((2, count, HD), BF16),
                vmem((rows, HD), BF16),
                vmem((rows, HD), BF16),
                vmem((HD, rows), BF16),
                vmem((HD, rows), BF16),
                vmem((n_resp, block, rows), F32),
                vmem((n_resp, block, rows), F32),
                vmem((n_resp, block, rows), BF16),
                vmem((count, rows), F32),
                vmem((count, rows), F32),
                vmem((count, rows), BF16),
                vmem((8, rows), F32),
                vmem((8, rows), F32),
                vmem((8, rows), F32),
                vmem((2, n_y, 2, half, HD), BF16),
                vmem((2, n_y, 2, half, HD), BF16),
                vmem((2, n_y, 2, half, HD), F32),
                vmem((2, n_y, half, HD), BF16),
                vmem((2, n_y, half, HD), BF16),
                vmem((2, n_y, half, HD), BF16),
                vmem((2, n_y, half, HD), BF16),
                vmem((2, half, HD), BF16),
                vmem((2, half, HD), BF16),
                vmem((n_tp, 16, HD), BF16),
                vmem((n_tp, 16, HD), BF16),
                vmem((2, count, HD), F32),
                vmem((n_resp * n_tp // 2, 16, HD), BF16),
                dma((4 + 2 * heads,)),
                dma((2,)),
                dma((2,)),
                dma((2,)),
                dma((2,)),
                dma((2, n_y)),
                dma((2, n_y)),
                dma((2, n_y)),
                dma((2, n_y)),
                dma((2, n_y)),
                dma((2, n_y)),
                dma((2,)),
                dma((2,)),
                dma((1,)),
                dma((1,)),
            ],
            compiler_params=pltpu.CompilerParams(
                collective_id=0, has_side_effects=True, vmem_limit_bytes=62 * 1024 * 1024
            ),
            cost_estimate=pl.CostEstimate(
                flops=10 * rows * (n_resp * block + count) * HD,
                bytes_accessed=4 * 1024 * 1024,
                transcendentals=rows * (n_resp * block + count),
            ),
        )(queries, resp_keys, resp_values, prefix_keys, prefix_values, cotangent, lengths)

    return jax.shard_map(
        per_device,
        mesh=mesh,
        in_specs=(
            P(("grp", "resp"), "tp"),
            P(("grp", "resp"), None),
            P(("grp", "resp"), None),
            P(("grp", "resp", "tp"), None),
            P(("grp", "resp", "tp"), None),
            P(("grp", "resp"), "tp"),
            P("grp"),
        ),
        out_specs=(
            P(("grp", "resp"), "tp"),
            P(("grp", "resp", "tp"), None),
            P(("grp", "resp", "tp"), None),
            P(("grp", "tp"), "resp"),
            P(("grp", "tp"), "resp"),
        ),
        check_vma=False,
    )
```

```python
import functools
import math

import jax
import jax.numpy as jnp
from jax import lax
from jax.experimental import pallas as pl
from jax.experimental.pallas import tpu as pltpu
from jax.sharding import PartitionSpec as P

MESH = pl.DeviceIdType.MESH
HD = 128
UNROLL = 4
F32 = jnp.float32
BF16 = jnp.bfloat16


def flip(value, bits):
    if bits & 1:
        value = value + 1 - 2 * lax.rem(value, 2)
    if bits & 2:
        value = value + 2 - 4 * lax.rem(value // 2, 2)
    return value


def fold(x, op):
    return op(x.reshape(x.shape[0] // 8, 8, x.shape[1]), axis=0)


def kernel(
    n_resp,
    n_tp,
    q_hbm,
    rk_hbm,
    rv_hbm,
    pk_hbm,
    pv_hbm,
    ct_hbm,
    len_ref,
    dq_ref,
    rdk_ref,
    rdv_ref,
    pdk_ref,
    pdv_ref,
    pin,
    kv,
    rkv,
    q_s,
    do_s,
    q_t,
    do_t,
    st,
    dp,
    pb,
    st_r,
    dp_r,
    pb_r,
    mx,
    sm,
    dl,
    sib_send,
    sib_recv,
    acc,
    z_send,
    z_recv,
    y_send,
    y_recv,
    p_send,
    p_recv,
    rg_send,
    rg_recv,
    rg_acc,
    sent,
    in_sem,
    a_send,
    a_recv,
    gs_send,
    gs_recv,
    fs_send,
    fs_recv,
    fz_send,
    fz_recv,
    fy_send,
    fy_recv,
    fp_send,
    fp_recv,
    rg_ssem,
    rg_rsem,
):
    r = lax.axis_index("resp")
    t = lax.axis_index("tp")
    n_y = n_resp // 2
    y, c = r // 2, lax.rem(r, 2)
    g, h = t // 2, lax.rem(t, 2)
    count = q_hbm.shape[0]
    heads = q_hbm.shape[1] // HD
    scale = 1.0 / math.sqrt(HD)
    block = kv.shape[2]
    half = block // 2

    sibling = {"resp": flip(r, 1), "tp": t}
    zpair = {"resp": r, "tp": flip(t, 1)}

    def yline(k):
        return {"resp": 2 * flip(y, k) + c, "tp": t}

    owner = {"resp": g, "tp": 2 * r + h}
    away = jnp.logical_not(r == g)

    def rcopy(src, dst, send, recv, dev):
        return pltpu.make_async_remote_copy(
            src_ref=src, dst_ref=dst, send_sem=send, recv_sem=recv, device_id=dev, device_id_type=MESH
        )

    col = pl.multiple_of(g * HD, HD)
    loads = [
        pltpu.make_async_copy(pk_hbm, pin.at[0], in_sem.at[0]),
        pltpu.make_async_copy(pv_hbm, pin.at[1], in_sem.at[1]),
        pltpu.make_async_copy(rk_hbm.at[:, pl.ds(col, HD)], rkv.at[0], in_sem.at[2]),
        pltpu.make_async_copy(rv_hbm.at[:, pl.ds(col, HD)], rkv.at[1], in_sem.at[3]),
    ]
    for j in range(heads):
        rows = pl.ds(j * count, count)
        loads.append(pltpu.make_async_copy(q_hbm.at[:, pl.ds(j * HD, HD)], q_s.at[rows], in_sem.at[4 + j]))
        loads.append(
            pltpu.make_async_copy(ct_hbm.at[:, pl.ds(j * HD, HD)], do_s.at[rows], in_sem.at[4 + heads + j])
        )
    for load in loads:
        load.start()

    n_z = n_tp // 2
    n_ring = 2 * n_y
    y_all, z = lax.rem(t, n_tp) // n_z * n_y + y, lax.rem(t, n_z)
    ys = [lax.rem(y_all + d, n_ring) for d in range(n_ring)]
    zs = [lax.rem(z + d, n_z) for d in range(n_z)]
    resp_of = [2 * lax.rem(v, n_y) + c for v in ys]
    tp_of = [v // n_y * n_z for v in ys]

    def hops(d, n):
        return min(d, n - d)

    offsets = [(i, j) for i in range(n_ring) for j in range(n_z) if i or j]
    offsets.sort(key=lambda o: -hops(o[0], n_ring) - hops(o[1], n_z))

    barrier = pltpu.get_barrier_semaphore()
    for i, j in offsets:
        pl.semaphore_signal(
            barrier, inc=1, device_id={"resp": resp_of[i], "tp": tp_of[i] + zs[j]}, device_id_type=MESH
        )
    pl.semaphore_signal(barrier, inc=1, device_id=sibling, device_id_type=MESH)

    @pl.when(away)
    def _():
        pl.semaphore_signal(barrier, inc=1, device_id=owner, device_id_type=MESH)

    for a in range(2):
        loads[a].wait()
    pl.semaphore_wait(barrier, len(offsets) + 1 + away.astype(jnp.int32))

    rows16 = pl.ds(pl.multiple_of(t * 16, 16), 16)
    spot = c * n_y + y
    for a in range(2):
        for i, j in offsets:
            to = tp_of[i] + zs[j]
            rcopy(
                pin.at[a, :, pl.ds(pl.multiple_of(to // 2 * HD, HD), HD)],
                kv.at[a, spot, rows16],
                a_send.at[a],
                a_recv.at[a],
                {"resp": resp_of[i], "tp": to},
            ).start()
        pltpu.make_async_copy(pin.at[a, :, pl.ds(col, HD)], kv.at[a, spot, rows16], a_recv.at[a]).start()

    for load in loads[2:]:
        load.wait()
    q_t[...] = jnp.transpose(q_s[...].astype(F32)).astype(BF16)
    length = len_ref[r]
    live = lax.rem(lax.broadcasted_iota(jnp.int32, do_s.shape, 0), count) < length
    masked = jnp.where(live, do_s[...].astype(F32), 0.0)
    do_s[...] = masked.astype(BF16)
    do_t[...] = jnp.transpose(masked).astype(BF16)

    s = jnp.dot(rkv[0], q_t[...], preferred_element_type=F32) * scale
    key_pos = lax.broadcasted_iota(jnp.int32, s.shape, 0)
    row_pos = lax.rem(lax.broadcasted_iota(jnp.int32, s.shape, 1), count)
    s = jnp.where(key_pos <= row_pos, s, -jnp.inf)
    st_r[...] = s
    mx[...] = fold(s, jnp.max)

    sends = []

    def start(copy):
        copy.start()
        sends.append(copy)

    near = pl.ds(c * n_y, n_y)
    far = pl.ds((1 - c) * n_y, n_y)

    def gather(a):
        pltpu.make_async_copy(kv.at[a, near], kv.at[a, near], a_recv.at[a]).wait()
        start(rcopy(kv.at[a, near], kv.at[a, near], gs_send.at[a], gs_recv.at[a], sibling))

    def gather_sib(a):
        rcopy(kv.at[a, far], kv.at[a, far], gs_send.at[a], gs_recv.at[a], sibling).wait_recv()

    def over(fn, first, blocks):
        lax.fori_loop(0, blocks, lambda i, carry: fn(first + i), None, unroll=UNROLL)

    def score(b):
        s = jnp.dot(kv[0, b], q_t[...], preferred_element_type=F32) * scale
        st[b] = s
        mx[...] = jnp.maximum(mx[...], fold(s, jnp.max))

    order = [k for k in (1, 3, 2) if k < n_y]
    gather(0)
    over(score, c * n_y, n_y)
    gather_sib(0)
    over(score, (1 - c) * n_y, n_y)

    mx[...] = jnp.broadcast_to(jnp.max(mx[...], axis=0, keepdims=True), mx.shape)
    def expo(x):
        x3 = x.reshape(x.shape[0] // 8, 8, x.shape[1])
        return jnp.exp(x3 - mx[...][None]).reshape(x.shape)

    def times(x, v):
        return (x.reshape(x.shape[0] // 8, 8, x.shape[1]) * v[None]).reshape(x.shape)

    def minus(x, v):
        return (x.reshape(x.shape[0] // 8, 8, x.shape[1]) - v[None]).reshape(x.shape)

    e = expo(st_r[...])
    st_r[...] = e
    sm[...] = fold(e, jnp.sum)

    def soften(b):
        e = expo(st[b])
        st[b] = e
        sm[...] += fold(e, jnp.sum)

    over(soften, 0, n_resp)
    sm[...] = jnp.broadcast_to(1.0 / jnp.sum(sm[...], axis=0, keepdims=True), sm.shape)

    def grad_out(a, b, keep, value):
        value = value.reshape(2, half, HD)
        if keep:
            acc[a, lax.rem(b, n_y)] = value
        else:
            sib_send[a, lax.rem(b, n_y)] = value.astype(BF16)

    def dv_block(b, keep):
        p = times(st[b], sm[...]).astype(BF16)
        pb[b] = p
        grad_out(1, b, keep, jnp.dot(p, do_s[...], preferred_element_type=F32))

    def dk_block(b, keep):
        ds = (times(st[b], sm[...]) * minus(dp[b], dl[...])).astype(BF16)
        pb[b] = ds
        grad_out(0, b, keep, jnp.dot(ds, q_s[...], preferred_element_type=F32) * scale)

    def grad_pass(a, fn):
        for k in range(n_y - 1, -1, -1):
            yy = flip(y, k)
            fn((1 - c) * n_y + yy, False)
            start(
                rcopy(
                    sib_send.at[a, yy], sib_recv.at[a, yy], fs_send.at[a, k], fs_recv.at[a, k], sibling
                )
            )
        for k in range(n_y - 1, -1, -1):
            yy = flip(y, k)
            fn(c * n_y + yy, True)
            rcopy(
                sib_send.at[a, yy], sib_recv.at[a, yy], fs_send.at[a, k], fs_recv.at[a, k], sibling
            ).wait_recv()
            z_send[a, k] = (acc[a, yy, 1 - h] + sib_recv[a, yy, 1 - h].astype(F32)).astype(BF16)
            start(rcopy(z_send.at[a, k], z_recv.at[a, k], fz_send.at[a, k], fz_recv.at[a, k], zpair))
            acc[a, yy, h] += sib_recv[a, yy, h].astype(F32)

    def sum_z(a):
        for k in range(n_y - 1, -1, -1):
            yy = flip(y, k)
            rcopy(z_send.at[a, k], z_recv.at[a, k], fz_send.at[a, k], fz_recv.at[a, k], zpair).wait_recv()
            total = acc[a, yy, h] + z_recv[a, k].astype(F32)
            if k:
                y_send[a, k] = total.astype(BF16)
                start(rcopy(y_send.at[a, k], y_recv.at[a, k], fy_send.at[a, k], fy_recv.at[a, k], yline(k)))
            else:
                acc[a, yy, h] = total

    def sum_y(a):
        total = acc[a, y, h]
        for k in order:
            rcopy(y_send.at[a, k], y_recv.at[a, k], fy_send.at[a, k], fy_recv.at[a, k], yline(k)).wait_recv()
            total = total + y_recv[a, k].astype(F32)
        p_send[a] = total.astype(BF16)
        home = rcopy(p_send.at[a], p_recv.at[a], fp_send.at[a], fp_recv.at[a], owner)
        local = pltpu.make_async_copy(p_send.at[a], p_recv.at[a], fp_recv.at[a])

        @pl.when(away)
        def _():
            home.start()

        @pl.when(r == g)
        def _():
            local.start()

        return home

    p = times(st_r[...], sm[...]).astype(BF16)
    pb_r[...] = p
    rg_acc[1] = jnp.dot(p, do_s[...], preferred_element_type=F32)
    grad_pass(1, dv_block)
    gather(1)

    d = jnp.dot(rkv[1], do_t[...], preferred_element_type=F32)
    dp_r[...] = d
    dl[...] = fold(pb_r[...].astype(F32) * d, jnp.sum)

    def dprob(b):
        d = jnp.dot(kv[1, b], do_t[...], preferred_element_type=F32)
        dp[b] = d
        dl[...] += fold(pb[b].astype(F32) * d, jnp.sum)

    over(dprob, c * n_y, n_y)
    sum_z(1)
    gather_sib(1)
    over(dprob, (1 - c) * n_y, n_y)
    dl[...] = jnp.broadcast_to(jnp.sum(dl[...], axis=0, keepdims=True), dl.shape)

    ds = (times(st_r[...], sm[...]) * minus(dp_r[...], dl[...])).astype(BF16)
    pb_r[...] = ds
    rg_acc[0] = jnp.dot(ds, q_s[...], preferred_element_type=F32) * scale
    own_rows = count // n_tp
    rg = jnp.concatenate(
        [rg_acc[0].reshape(n_tp, own_rows, HD), rg_acc[1].reshape(n_tp, own_rows, HD)], axis=1
    )
    rg_send[...] = rg.astype(BF16)

    def spread(d, carry):
        to = lax.rem(t + d, n_tp)
        rcopy(rg_send.at[to], rg_recv.at[t], rg_ssem.at[0], rg_rsem.at[0], {"resp": r, "tp": to}).start()
        return carry

    lax.fori_loop(1, n_tp, spread, 0)
    pltpu.make_async_copy(rg_send.at[t], rg_recv.at[t], rg_rsem.at[0]).start()

    grad_pass(0, dk_block)
    home_v = sum_y(1)

    def tdot(a, b):
        return lax.dot_general(a, b, (((0,), (0,)), ((), ())), preferred_element_type=F32)

    dq_t = tdot(rkv[0], pb_r[...]) + tdot(kv[0].reshape(n_resp * block, HD), pb[...].reshape(n_resp * block, heads * count))
    for j in range(heads):
        dq_ref[:, j * HD : (j + 1) * HD] = jnp.transpose(dq_t[:, j * count : (j + 1) * count]) * scale
    sum_z(0)

    pltpu.make_async_copy(rg_recv, rg_recv, rg_rsem.at[0]).wait()
    got = rg_recv[...].astype(F32)
    for i in range(n_tp // 2):
        both = got[2 * i] + got[2 * i + 1]
        rdk_ref[:, i * HD : (i + 1) * HD] = both[:own_rows]
        rdv_ref[:, i * HD : (i + 1) * HD] = both[own_rows:]

    home_k = sum_y(0)
    home_v.wait_recv()
    pdv_ref[...] = p_recv[1].astype(F32)
    home_k.wait_recv()
    pdk_ref[...] = p_recv[0].astype(F32)

    for a in range(2):
        pltpu.make_async_copy(
            sent.at[pl.ds(0, len(offsets))], sent.at[pl.ds(0, len(offsets))], a_send.at[a]
        ).wait()
    pltpu.make_async_copy(
        rg_send.at[pl.ds(0, n_tp - 1)], rg_send.at[pl.ds(0, n_tp - 1)], rg_ssem.at[0]
    ).wait()
    for copy in sends:
        copy.wait_send()

    @pl.when(away)
    def _():
        home_v.wait_send()
        home_k.wait_send()


def write_out(*refs):
    sem = refs[10]
    copies = [pltpu.make_async_copy(refs[i], refs[5 + i], sem.at[i]) for i in range(5)]
    for copy in copies:
        copy.start()
    for copy in copies:
        copy.wait()


def solution(mesh):
    n_resp, n_tp = mesh.shape["resp"], mesh.shape["tp"]
    n_y = n_resp // 2

    def per_device(queries, resp_keys, resp_values, prefix_keys, prefix_values, cotangent, lengths):
        count, width = queries.shape
        heads = width // HD
        rows = heads * count
        block = n_tp * prefix_keys.shape[0]
        half = block // 2
        cols = prefix_keys.shape[1]
        dma = pltpu.SemaphoreType.DMA
        vmem = pltpu.VMEM
        any_spec = pl.BlockSpec(memory_space=pl.ANY)
        vmem_spec = pl.BlockSpec(memory_space=pltpu.VMEM)
        shapes = ((count, width), (count // n_tp, cols), (count // n_tp, cols), (half, HD), (half, HD))
        results = pl.pallas_call(
            functools.partial(kernel, n_resp, n_tp),
            out_shape=tuple(pltpu.VMEM(shape, F32) for shape in shapes),
            in_specs=[any_spec] * 6 + [pl.BlockSpec(memory_space=pltpu.SMEM)],
            out_specs=(vmem_spec,) * 5,
            scratch_shapes=[
                vmem((2, 16, cols), BF16),
                vmem((2, n_resp, block, HD), BF16),
                vmem((2, count, HD), BF16),
                vmem((rows, HD), BF16),
                vmem((rows, HD), BF16),
                vmem((HD, rows), BF16),
                vmem((HD, rows), BF16),
                vmem((n_resp, block, rows), F32),
                vmem((n_resp, block, rows), F32),
                vmem((n_resp, block, rows), BF16),
                vmem((count, rows), F32),
                vmem((count, rows), F32),
                vmem((count, rows), BF16),
                vmem((8, rows), F32),
                vmem((8, rows), F32),
                vmem((8, rows), F32),
                vmem((2, n_y, 2, half, HD), BF16),
                vmem((2, n_y, 2, half, HD), BF16),
                vmem((2, n_y, 2, half, HD), F32),
                vmem((2, n_y, half, HD), BF16),
                vmem((2, n_y, half, HD), BF16),
                vmem((2, n_y, half, HD), BF16),
                vmem((2, n_y, half, HD), BF16),
                vmem((2, half, HD), BF16),
                vmem((2, half, HD), BF16),
                vmem((n_tp, 16, HD), BF16),
                vmem((n_tp, 16, HD), BF16),
                vmem((2, count, HD), F32),
                vmem((n_resp * n_tp // 2, 16, HD), BF16),
                dma((4 + 2 * heads,)),
                dma((2,)),
                dma((2,)),
                dma((2,)),
                dma((2,)),
                dma((2, n_y)),
                dma((2, n_y)),
                dma((2, n_y)),
                dma((2, n_y)),
                dma((2, n_y)),
                dma((2, n_y)),
                dma((2,)),
                dma((2,)),
                dma((1,)),
                dma((1,)),
            ],
            compiler_params=pltpu.CompilerParams(
                collective_id=0, has_side_effects=True, vmem_limit_bytes=62 * 1024 * 1024
            ),
            cost_estimate=pl.CostEstimate(
                flops=10 * rows * (n_resp * block + count) * HD,
                bytes_accessed=4 * 1024 * 1024,
                transcendentals=rows * (n_resp * block + count),
            ),
        )(queries, resp_keys, resp_values, prefix_keys, prefix_values, cotangent, lengths)
        return pl.pallas_call(
            write_out,
            out_shape=tuple(jax.ShapeDtypeStruct(shape, F32) for shape in shapes),
            in_specs=[any_spec] * 5,
            out_specs=(any_spec,) * 5,
            scratch_shapes=[dma((5,))],
        )(*results)

    return jax.shard_map(
        per_device,
        mesh=mesh,
        in_specs=(
            P(("grp", "resp"), "tp"),
            P(("grp", "resp"), None),
            P(("grp", "resp"), None),
            P(("grp", "resp", "tp"), None),
            P(("grp", "resp", "tp"), None),
            P(("grp", "resp"), "tp"),
            P("grp"),
        ),
        out_specs=(
            P(("grp", "resp"), "tp"),
            P(("grp", "resp", "tp"), None),
            P(("grp", "resp", "tp"), None),
            P(("grp", "tp"), "resp"),
            P(("grp", "tp"), "resp"),
        ),
        check_vma=False,
    )
```

```python
import functools
import math

import jax
import jax.numpy as jnp
from jax import lax
from jax.experimental import pallas as pl
from jax.experimental.pallas import tpu as pltpu
from jax.sharding import PartitionSpec as P

MESH = pl.DeviceIdType.MESH
HD = 128
UNROLL = 4
F32 = jnp.float32
BF16 = jnp.bfloat16


def flip(value, bits):
    if bits & 1:
        value = value + 1 - 2 * lax.rem(value, 2)
    if bits & 2:
        value = value + 2 - 4 * lax.rem(value // 2, 2)
    return value


def fold(x, op):
    return op(x.reshape(x.shape[0] // 8, 8, x.shape[1]), axis=0)


def kernel(
    n_resp,
    n_tp,
    q_hbm,
    rk_hbm,
    rv_hbm,
    pk_hbm,
    pv_hbm,
    ct_hbm,
    len_ref,
    dq_ref,
    rdk_ref,
    rdv_ref,
    pdk_ref,
    pdv_ref,
    pin,
    kv,
    rkv,
    q_s,
    do_s,
    q_t,
    do_t,
    st,
    dp,
    pb,
    st_r,
    dp_r,
    pb_r,
    mx,
    sm,
    dl,
    sib_send,
    sib_recv,
    acc,
    z_send,
    z_recv,
    y_send,
    y_recv,
    p_send,
    p_recv,
    rg_send,
    rg_recv,
    rg_acc,
    sent,
    in_sem,
    a_send,
    a_recv,
    gs_send,
    gs_recv,
    fs_send,
    fs_recv,
    fz_send,
    fz_recv,
    fy_send,
    fy_recv,
    fp_send,
    fp_recv,
    rg_ssem,
    rg_rsem,
):
    r = lax.axis_index("resp")
    t = lax.axis_index("tp")
    n_y = n_resp // 2
    y, c = r // 2, lax.rem(r, 2)
    g, h = t // 2, lax.rem(t, 2)
    count = q_hbm.shape[0]
    heads = q_hbm.shape[1] // HD
    scale = 1.0 / math.sqrt(HD)
    block = kv.shape[2]
    half = block // 2

    sibling = {"resp": flip(r, 1), "tp": t}
    zpair = {"resp": r, "tp": flip(t, 1)}

    def yline(k):
        return {"resp": 2 * flip(y, k) + c, "tp": t}

    owner = {"resp": g, "tp": 2 * r + h}
    away = jnp.logical_not(r == g)

    def rcopy(src, dst, send, recv, dev):
        return pltpu.make_async_remote_copy(
            src_ref=src, dst_ref=dst, send_sem=send, recv_sem=recv, device_id=dev, device_id_type=MESH
        )

    col = pl.multiple_of(g * HD, HD)
    loads = [
        pltpu.make_async_copy(pk_hbm, pin.at[0], in_sem.at[0]),
        pltpu.make_async_copy(pv_hbm, pin.at[1], in_sem.at[1]),
        pltpu.make_async_copy(rk_hbm.at[:, pl.ds(col, HD)], rkv.at[0], in_sem.at[2]),
        pltpu.make_async_copy(rv_hbm.at[:, pl.ds(col, HD)], rkv.at[1], in_sem.at[3]),
    ]
    for j in range(heads):
        rows = pl.ds(j * count, count)
        loads.append(pltpu.make_async_copy(q_hbm.at[:, pl.ds(j * HD, HD)], q_s.at[rows], in_sem.at[4 + j]))
        loads.append(
            pltpu.make_async_copy(ct_hbm.at[:, pl.ds(j * HD, HD)], do_s.at[rows], in_sem.at[4 + heads + j])
        )
    for load in loads:
        load.start()

    n_z = n_tp // 2
    n_ring = 2 * n_y
    y_all, z = lax.rem(t, n_tp) // n_z * n_y + y, lax.rem(t, n_z)
    ys = [lax.rem(y_all + d, n_ring) for d in range(n_ring)]
    zs = [lax.rem(z + d, n_z) for d in range(n_z)]
    resp_of = [2 * lax.rem(v, n_y) + c for v in ys]
    tp_of = [v // n_y * n_z for v in ys]

    def hops(d, n):
        return min(d, n - d)

    offsets = [(i, j) for i in range(n_ring) for j in range(n_z) if i or j]
    offsets.sort(key=lambda o: -hops(o[0], n_ring) - hops(o[1], n_z))
    classes = sorted(range(n_y), key=lambda v: -hops(v, n_ring) - hops(v + n_y, n_ring) - 8 * (v == 0) + 8 * (v == n_y // 2))

    barrier = pltpu.get_barrier_semaphore()
    for i, j in offsets:
        pl.semaphore_signal(
            barrier, inc=1, device_id={"resp": resp_of[i], "tp": tp_of[i] + zs[j]}, device_id_type=MESH
        )
    pl.semaphore_signal(barrier, inc=1, device_id=sibling, device_id_type=MESH)

    @pl.when(away)
    def _():
        pl.semaphore_signal(barrier, inc=1, device_id=owner, device_id_type=MESH)

    for a in range(2):
        loads[a].wait()
    pl.semaphore_wait(barrier, len(offsets) + 1 + away.astype(jnp.int32))

    rows16 = pl.ds(pl.multiple_of(t * 16, 16), 16)
    spot = c * n_y + y
    for a in range(2):
        for v in classes:
            for i, j in offsets:
                if i % n_y == v:
                    to = tp_of[i] + zs[j]
                    rcopy(
                        pin.at[a, :, pl.ds(pl.multiple_of(to // 2 * HD, HD), HD)],
                        kv.at[a, spot, rows16],
                        a_send.at[a],
                        a_recv.at[a, v],
                        {"resp": resp_of[i], "tp": to},
                    ).start()
            if v == 0:
                pltpu.make_async_copy(
                    pin.at[a, :, pl.ds(col, HD)], kv.at[a, spot, rows16], a_recv.at[a, 0]
                ).start()

    for load in loads[2:]:
        load.wait()
    q_t[...] = jnp.transpose(q_s[...].astype(F32)).astype(BF16)
    length = len_ref[r]
    live = lax.rem(lax.broadcasted_iota(jnp.int32, do_s.shape, 0), count) < length
    masked = jnp.where(live, do_s[...].astype(F32), 0.0)
    do_s[...] = masked.astype(BF16)
    do_t[...] = jnp.transpose(masked).astype(BF16)

    s = jnp.dot(rkv[0], q_t[...], preferred_element_type=F32) * scale
    key_pos = lax.broadcasted_iota(jnp.int32, s.shape, 0)
    row_pos = lax.rem(lax.broadcasted_iota(jnp.int32, s.shape, 1), count)
    s = jnp.where(key_pos <= row_pos, s, -jnp.inf)
    st_r[...] = s
    mx[...] = fold(s, jnp.max)

    sends, homes = [], []

    def start(copy):
        copy.start()
        sends.append(copy)

    def near(v):
        return c * n_y + lax.rem(y + n_y - v, n_y)

    def far(v):
        return (1 - c) * n_y + lax.rem(y + n_y - v, n_y)

    def gather(a, fn):
        def from_sibling(v):
            ref = kv.at[a, far(v)]
            rcopy(ref, ref, gs_send.at[a, v], gs_recv.at[a, v], sibling).wait_recv()
            fn(far(v))

        for n, v in enumerate(classes):
            ref = kv.at[a, near(v)]
            pltpu.make_async_copy(ref, ref, a_recv.at[a, v]).wait()
            start(rcopy(ref, ref, gs_send.at[a, v], gs_recv.at[a, v], sibling))
            fn(near(v))
            if n:
                from_sibling(classes[n - 1])
        from_sibling(classes[-1])

    def over(fn, first, blocks):
        lax.fori_loop(0, blocks, lambda i, carry: fn(first + i), None, unroll=UNROLL)

    def score(b):
        s = jnp.dot(kv[0, b], q_t[...], preferred_element_type=F32) * scale
        st[b] = s
        mx[...] = jnp.maximum(mx[...], fold(s, jnp.max))

    gather(0, score)

    mx[...] = jnp.broadcast_to(jnp.max(mx[...], axis=0, keepdims=True), mx.shape)
    def expo(x):
        x3 = x.reshape(x.shape[0] // 8, 8, x.shape[1])
        return jnp.exp(x3 - mx[...][None]).reshape(x.shape)

    def times(x, v):
        return (x.reshape(x.shape[0] // 8, 8, x.shape[1]) * v[None]).reshape(x.shape)

    def minus(x, v):
        return (x.reshape(x.shape[0] // 8, 8, x.shape[1]) - v[None]).reshape(x.shape)

    e = expo(st_r[...])
    st_r[...] = e
    sm[...] = fold(e, jnp.sum)

    def soften(b):
        e = expo(st[b])
        st[b] = e
        sm[...] += fold(e, jnp.sum)

    over(soften, 0, n_resp)
    sm[...] = jnp.broadcast_to(1.0 / jnp.sum(sm[...], axis=0, keepdims=True), sm.shape)

    def grad_out(a, b, keep, value):
        value = value.reshape(2, half, HD)
        if keep:
            acc[a, lax.rem(b, n_y)] = value
        else:
            sib_send[a, lax.rem(b, n_y)] = value.astype(BF16)

    def dv_block(b, keep):
        p = times(st[b], sm[...]).astype(BF16)
        pb[b] = p
        grad_out(1, b, keep, jnp.dot(p, do_s[...], preferred_element_type=F32))

    def dk_block(b, keep):
        ds = (times(st[b], sm[...]) * minus(dp[b], dl[...])).astype(BF16)
        pb[b] = ds
        grad_out(0, b, keep, jnp.dot(ds, q_s[...], preferred_element_type=F32) * scale)

    def grad_pass(a, fn):
        for k in range(n_y - 1, -1, -1):
            yy = flip(y, k)
            fn((1 - c) * n_y + yy, False)
            start(
                rcopy(
                    sib_send.at[a, yy], sib_recv.at[a, yy], fs_send.at[a, k], fs_recv.at[a, k], sibling
                )
            )
        for k in range(n_y - 1, -1, -1):
            yy = flip(y, k)
            fn(c * n_y + yy, True)
            rcopy(
                sib_send.at[a, yy], sib_recv.at[a, yy], fs_send.at[a, k], fs_recv.at[a, k], sibling
            ).wait_recv()
            z_send[a, k] = (acc[a, yy, 1 - h] + sib_recv[a, yy, 1 - h].astype(F32)).astype(BF16)
            start(rcopy(z_send.at[a, k], z_recv.at[a, k], fz_send.at[a, k], fz_recv.at[a, k], zpair))
            acc[a, yy, h] += sib_recv[a, yy, h].astype(F32)

    def sum_z(a):
        for k in range(n_y - 1, -1, -1):
            yy = flip(y, k)
            rcopy(z_send.at[a, k], z_recv.at[a, k], fz_send.at[a, k], fz_recv.at[a, k], zpair).wait_recv()
            total = acc[a, yy, h] + z_recv[a, k].astype(F32)
            if k:
                y_send[a, k] = total.astype(BF16)
                start(rcopy(y_send.at[a, k], y_recv.at[a, k], fy_send.at[a, k], fy_recv.at[a, k], yline(k)))
            else:
                acc[a, yy, h] = total

    def sum_y(a):
        total = acc[a, y, h]
        for k in (1, 3, 2):
            rcopy(y_send.at[a, k], y_recv.at[a, k], fy_send.at[a, k], fy_recv.at[a, k], yline(k)).wait_recv()
            total = total + y_recv[a, k].astype(F32)
        p_send[a] = total.astype(BF16)
        home = rcopy(p_send.at[a], p_recv.at[a], fp_send.at[a], fp_recv.at[a], owner)
        local = pltpu.make_async_copy(p_send.at[a], p_recv.at[a], fp_recv.at[a])
        pl.when(away)(home.start)
        pl.when(r == g)(local.start)
        homes.append(home)

    p = times(st_r[...], sm[...]).astype(BF16)
    pb_r[...] = p
    rg_acc[1] = jnp.dot(p, do_s[...], preferred_element_type=F32)
    grad_pass(1, dv_block)
    d = jnp.dot(rkv[1], do_t[...], preferred_element_type=F32)
    dp_r[...] = d
    dl[...] = fold(pb_r[...].astype(F32) * d, jnp.sum)

    def dprob(b):
        d = jnp.dot(kv[1, b], do_t[...], preferred_element_type=F32)
        dp[b] = d
        dl[...] += fold(pb[b].astype(F32) * d, jnp.sum)

    gather(1, dprob)
    sum_z(1)
    dl[...] = jnp.broadcast_to(jnp.sum(dl[...], axis=0, keepdims=True), dl.shape)

    grad_pass(0, dk_block)
    ds = (times(st_r[...], sm[...]) * minus(dp_r[...], dl[...])).astype(BF16)
    pb_r[...] = ds
    rg_acc[0] = jnp.dot(ds, q_s[...], preferred_element_type=F32) * scale
    own_rows = count // n_tp
    rg = jnp.concatenate(
        [rg_acc[0].reshape(n_tp, own_rows, HD), rg_acc[1].reshape(n_tp, own_rows, HD)], axis=1
    )
    rg_send[...] = rg.astype(BF16)

    def spread(d, carry):
        to = lax.rem(t + d, n_tp)
        rcopy(rg_send.at[to], rg_recv.at[t], rg_ssem.at[0], rg_rsem.at[0], {"resp": r, "tp": to}).start()
        return carry

    lax.fori_loop(1, n_tp, spread, 0)
    pltpu.make_async_copy(rg_send.at[t], rg_recv.at[t], rg_rsem.at[0]).start()


    sum_y(1)

    def tdot(a, b):
        return lax.dot_general(a, b, (((0,), (0,)), ((), ())), preferred_element_type=F32)

    dq_t = tdot(rkv[0], pb_r[...]) + tdot(kv[0].reshape(n_resp * block, HD), pb[...].reshape(n_resp * block, heads * count))
    for j in range(heads):
        dq_ref[:, j * HD : (j + 1) * HD] = jnp.transpose(dq_t[:, j * count : (j + 1) * count]) * scale
    sum_z(0)

    pltpu.make_async_copy(rg_recv, rg_recv, rg_rsem.at[0]).wait()
    got = rg_recv[...].astype(F32)
    for i in range(n_tp // 2):
        both = got[2 * i] + got[2 * i + 1]
        rdk_ref[:, i * HD : (i + 1) * HD] = both[:own_rows]
        rdv_ref[:, i * HD : (i + 1) * HD] = both[own_rows:]

    sum_y(0)
    homes[0].wait_recv()
    pdv_ref[...] = p_recv[1].astype(F32)
    homes[1].wait_recv()
    pdk_ref[...] = p_recv[0].astype(F32)

    for a in range(2):
        pltpu.make_async_copy(
            sent.at[pl.ds(0, len(offsets))], sent.at[pl.ds(0, len(offsets))], a_send.at[a]
        ).wait()
    pltpu.make_async_copy(
        rg_send.at[pl.ds(0, n_tp - 1)], rg_send.at[pl.ds(0, n_tp - 1)], rg_ssem.at[0]
    ).wait()
    for copy in sends:
        copy.wait_send()

    @pl.when(away)
    def _():
        for home in homes:
            home.wait_send()


def write_out(*refs):
    sem = refs[10]
    copies = [pltpu.make_async_copy(refs[i], refs[5 + i], sem.at[i]) for i in range(5)]
    for copy in copies:
        copy.start()
    for copy in copies:
        copy.wait()


def solution(mesh):
    n_resp, n_tp = mesh.shape["resp"], mesh.shape["tp"]
    n_y = n_resp // 2

    def per_device(queries, resp_keys, resp_values, prefix_keys, prefix_values, cotangent, lengths):
        count, width = queries.shape
        heads = width // HD
        rows = heads * count
        block = n_tp * prefix_keys.shape[0]
        half = block // 2
        cols = prefix_keys.shape[1]
        dma = pltpu.SemaphoreType.DMA
        vmem = pltpu.VMEM
        any_spec = pl.BlockSpec(memory_space=pl.ANY)
        vmem_spec = pl.BlockSpec(memory_space=pltpu.VMEM)
        shapes = ((count, width), (count // n_tp, cols), (count // n_tp, cols), (half, HD), (half, HD))
        results = pl.pallas_call(
            functools.partial(kernel, n_resp, n_tp),
            out_shape=tuple(pltpu.VMEM(shape, F32) for shape in shapes),
            in_specs=[any_spec] * 6 + [pl.BlockSpec(memory_space=pltpu.SMEM)],
            out_specs=(vmem_spec,) * 5,
            scratch_shapes=[
                vmem((2, 16, cols), BF16),
                vmem((2, n_resp, block, HD), BF16),
                vmem((2, count, HD), BF16),
                vmem((rows, HD), BF16),
                vmem((rows, HD), BF16),
                vmem((HD, rows), BF16),
                vmem((HD, rows), BF16),
                vmem((n_resp, block, rows), F32),
                vmem((n_resp, block, rows), F32),
                vmem((n_resp, block, rows), BF16),
                vmem((count, rows), F32),
                vmem((count, rows), F32),
                vmem((count, rows), BF16),
                vmem((8, rows), F32),
                vmem((8, rows), F32),
                vmem((8, rows), F32),
                vmem((2, n_y, 2, half, HD), BF16),
                vmem((2, n_y, 2, half, HD), BF16),
                vmem((2, n_y, 2, half, HD), F32),
                vmem((2, n_y, half, HD), BF16),
                vmem((2, n_y, half, HD), BF16),
                vmem((2, n_y, half, HD), BF16),
                vmem((2, n_y, half, HD), BF16),
                vmem((2, half, HD), BF16),
                vmem((2, half, HD), BF16),
                vmem((n_tp, 16, HD), BF16),
                vmem((n_tp, 16, HD), BF16),
                vmem((2, count, HD), F32),
                vmem((n_resp * n_tp // 2, 16, HD), BF16),
                dma((4 + 2 * heads,)),
                dma((2,)),
                dma((2, n_y)),
                dma((2, n_y)),
                dma((2, n_y)),
                dma((2, n_y)),
                dma((2, n_y)),
                dma((2, n_y)),
                dma((2, n_y)),
                dma((2, n_y)),
                dma((2, n_y)),
                dma((2,)),
                dma((2,)),
                dma((1,)),
                dma((1,)),
            ],
            compiler_params=pltpu.CompilerParams(
                collective_id=0, has_side_effects=True, vmem_limit_bytes=62 * 1024 * 1024
            ),
            cost_estimate=pl.CostEstimate(
                flops=10 * rows * (n_resp * block + count) * HD,
                bytes_accessed=4 * 1024 * 1024,
                transcendentals=rows * (n_resp * block + count),
            ),
        )(queries, resp_keys, resp_values, prefix_keys, prefix_values, cotangent, lengths)
        return pl.pallas_call(
            write_out,
            out_shape=tuple(jax.ShapeDtypeStruct(shape, F32) for shape in shapes),
            in_specs=[any_spec] * 5,
            out_specs=(any_spec,) * 5,
            scratch_shapes=[dma((5,))],
            compiler_params=pltpu.CompilerParams(vmem_limit_bytes=256 * 1024),
        )(*results)

    return jax.shard_map(
        per_device,
        mesh=mesh,
        in_specs=(
            P(("grp", "resp"), "tp"),
            P(("grp", "resp"), None),
            P(("grp", "resp"), None),
            P(("grp", "resp", "tp"), None),
            P(("grp", "resp", "tp"), None),
            P(("grp", "resp"), "tp"),
            P("grp"),
        ),
        out_specs=(
            P(("grp", "resp"), "tp"),
            P(("grp", "resp", "tp"), None),
            P(("grp", "resp", "tp"), None),
            P(("grp", "tp"), "resp"),
            P(("grp", "tp"), "resp"),
        ),
        check_vma=False,
    )
```

```python
import functools
import math

import jax
import jax.numpy as jnp
from jax import lax
from jax.experimental import pallas as pl
from jax.experimental.pallas import tpu as pltpu
from jax.sharding import PartitionSpec as P

MESH = pl.DeviceIdType.MESH
HD = 128
TILE = 16
F32 = jnp.float32
BF16 = jnp.bfloat16


def flip(value, bits):
    if bits & 1:
        value = value + 1 - 2 * lax.rem(value, 2)
    if bits & 2:
        value = value + 2 - 4 * lax.rem(value // 2, 2)
    return value


def fold(x, op):
    return op(x.reshape(x.shape[0] // 8, 8, x.shape[1]), axis=0)


def by_row(x, v, op):
    return op(x.reshape(x.shape[0] // 8, 8, x.shape[1]), v[None]).reshape(x.shape)


def kernel(
    n_resp,
    n_tp,
    q_hbm,
    rk_hbm,
    rv_hbm,
    pk_hbm,
    pv_hbm,
    ct_hbm,
    len_ref,
    dq_ref,
    rdk_ref,
    rdv_ref,
    pdk_ref,
    pdv_ref,
    pin,
    kv,
    rkv,
    qd,
    qd_t,
    st,
    dp,
    pb,
    st_r,
    dp_r,
    pb_r,
    mx,
    sm,
    dl,
    stat_send,
    stat_recv,
    del_send,
    del_recv,
    acc,
    y_send,
    y_recv,
    p_send,
    p_recv,
    rg_send,
    rg_recv,
    rg_acc,
    dqs_send,
    dqs_recv,
    dqz_send,
    dqz_recv,
    sent,
    in_sem,
    a_send,
    a_recv,
    xq_send,
    xq_recv,
    st_ssem,
    st_rsem,
    de_ssem,
    de_rsem,
    fy_send,
    fy_recv,
    fp_send,
    fp_recv,
    rg_ssem,
    rg_rsem,
    dq_ssem,
    dq_rsem,
):
    r = lax.axis_index("resp")
    t = lax.axis_index("tp")
    n_y = n_resp // 2
    n_z = n_tp // 2
    n_ring = 2 * n_y
    y, c = r // 2, lax.rem(r, 2)
    g, h = t // 2, lax.rem(t, 2)
    y_hi, z = t // n_z, lax.rem(t, n_z)
    count = q_hbm.shape[0]
    heads = q_hbm.shape[1] // HD
    rows = heads * count
    scale = 1.0 / math.sqrt(HD)

    def rcopy(src, dst, send, recv, dev):
        return pltpu.make_async_remote_copy(
            src_ref=src, dst_ref=dst, send_sem=send, recv_sem=recv, device_id=dev, device_id_type=MESH
        )

    sends = []

    def start(copy):
        copy.start()
        sends.append(copy)

    def mate(m):
        return {"resp": flip(r, m & 1), "tp": flip(t, m >> 1)}

    def yline(k):
        return {"resp": 2 * flip(y, k) + c, "tp": t}

    def owner(k):
        return {"resp": g, "tp": 2 * r + k}

    def own(k):
        return jnp.logical_and(r == g, h == k)

    ys = [lax.rem(y_hi * n_y + y + d, n_ring) for d in range(n_ring)]
    resp_of = [2 * lax.rem(v, n_y) + c for v in ys]
    tp_of = [v // n_y * n_z for v in ys]
    sign = 1 - 2 * h
    z_to = [lax.rem(z + sign * d + n_z, n_z) for d in (0, -1, 2, -3)]
    z_from = [lax.rem(z - sign * d + n_z, n_z) for d in range(4)]

    def hops(d):
        return min(d, n_ring - d)

    offsets = [(i, j) for i in range(n_ring) for j in range(4) if i or j]
    offsets.sort(key=lambda o: -hops(o[0]) - o[1])
    classes = (0, 1, 3, 2)

    barrier = pltpu.get_barrier_semaphore()
    for i, j in offsets:
        pl.semaphore_signal(
            barrier, inc=1, device_id={"resp": resp_of[i], "tp": tp_of[i] + z_from[j]}, device_id_type=MESH
        )

    def greet(d, carry):
        pl.semaphore_signal(
            barrier, inc=1, device_id={"resp": r, "tp": lax.rem(t + d, n_tp)}, device_id_type=MESH
        )
        return carry

    lax.fori_loop(1, n_tp, greet, 0)
    for m in (1, 3):
        pl.semaphore_signal(barrier, inc=1, device_id=mate(m), device_id_type=MESH)
    for k in range(2):

        @pl.when(jnp.logical_not(own(k)))
        def _(k=k):
            pl.semaphore_signal(barrier, inc=1, device_id=owner(k), device_id_type=MESH)

    col = pl.multiple_of(g * HD, HD)
    loads = [
        pltpu.make_async_copy(pk_hbm, pin.at[0], in_sem.at[0]),
        pltpu.make_async_copy(pv_hbm, pin.at[1], in_sem.at[1]),
        pltpu.make_async_copy(rk_hbm.at[:, pl.ds(col, HD)], rkv.at[0], in_sem.at[2]),
        pltpu.make_async_copy(rv_hbm.at[:, pl.ds(col, HD)], rkv.at[1], in_sem.at[3]),
    ]
    for i, ref in enumerate((q_hbm, ct_hbm)):
        for j in range(heads):
            loads.append(
                pltpu.make_async_copy(
                    ref.at[:, pl.ds(j * HD, HD)], qd.at[i, 0, pl.ds(j * count, count)], in_sem.at[4 + heads * i + j]
                )
            )
    for load in loads:
        load.start()
    loads[0].wait()
    for load in loads[4 : 4 + heads]:
        load.wait()
    same = (r == g).astype(jnp.int32)
    pl.semaphore_wait(barrier, len(offsets) + n_tp - 1 + 2 + 2 - same)

    def share(i):
        for m in (2, 1):
            start(rcopy(qd.at[i, 0], qd.at[i, m], xq_send.at[i, m], xq_recv.at[i, m], mate(m)))

    def shared(i, m):
        rcopy(qd.at[i, m], qd.at[i, m], xq_send.at[i, m], xq_recv.at[i, m], mate(m)).wait_recv()

    def relay(i):
        shared(i, 2)
        start(rcopy(qd.at[i, 2], qd.at[i, 3], xq_send.at[i, 3], xq_recv.at[i, 3], mate(1)))

    def turn(i, m):
        qd_t[i, m] = jnp.transpose(qd[i, m].astype(F32)).astype(BF16)

    def scatter(a):
        for v in classes:
            for i, j in [o for o in offsets if o[0] % n_y == v] + [(0, 0)] * (v == 0):
                to = tp_of[i] + z_to[j]
                slot = pl.ds(pl.multiple_of(y_hi * 4 * TILE + j * TILE, TILE), TILE)
                src = pin.at[a, :, pl.ds(pl.multiple_of(to // 2 * HD, HD), HD)]
                dst = kv.at[a, y, slot]
                if i or j:
                    rcopy(src, dst, a_send.at[a], a_recv.at[a, v], {"resp": resp_of[i], "tp": to}).start()
                else:
                    pltpu.make_async_copy(src, dst, a_recv.at[a, v]).start()

    share(0)
    scatter(0)
    for load in loads[4 + heads :]:
        load.wait()
    length = len_ref[r]
    live = lax.rem(lax.broadcasted_iota(jnp.int32, (rows, HD), 0), count) < length
    qd[1, 0] = jnp.where(live, qd[1, 0].astype(F32), 0.0).astype(BF16)
    share(1)
    for load in loads[1:4]:
        load.wait()
    scatter(1)

    turn(0, 0)
    s = jnp.dot(rkv[0], qd_t[0, 0], preferred_element_type=F32) * scale
    key_pos = lax.broadcasted_iota(jnp.int32, s.shape, 0)
    row_pos = lax.rem(lax.broadcasted_iota(jnp.int32, s.shape, 1), count)
    s = jnp.where(key_pos <= row_pos, s, -jnp.inf)
    st_r[...] = s
    mx[0] = fold(s, jnp.max)
    for m in range(1, 4):
        mx[m] = jnp.full((8, rows), -jnp.inf, F32)
    turn(1, 0)

    relay(0)
    turn(0, 2)
    shared(0, 1)
    turn(0, 1)
    shared(0, 3)
    turn(0, 3)

    def arrived(a, v):
        b = lax.rem(y + n_y - v, n_y)
        pltpu.make_async_copy(kv.at[a, b], kv.at[a, b], a_recv.at[a, v]).wait()
        return b

    for n, v in enumerate(classes):
        b = arrived(0, v)
        for m in range(4):
            s = jnp.dot(kv[0, b], qd_t[0, m], preferred_element_type=F32) * scale
            st[b, m] = s
            mx[m] = jnp.maximum(mx[m], fold(s, jnp.max))
        if n == 0:
            relay(1)

    for m in range(4):
        top = jnp.max(mx[m], axis=0, keepdims=True)
        stat_send[0, m] = top
        mx[m] = jnp.broadcast_to(top, (8, rows))
    e = jnp.exp(by_row(st_r[...], mx[0], jnp.subtract))
    st_r[...] = e
    sm[0] = fold(e, jnp.sum)
    for m in range(1, 4):
        sm[m] = jnp.zeros((8, rows), F32)

    def soften(b, carry):
        for m in range(4):
            e = jnp.exp(by_row(st[b, m], mx[m], jnp.subtract))
            st[b, m] = e
            sm[m] += fold(e, jnp.sum)
        return carry

    lax.fori_loop(0, n_y, soften, 0, unroll=True)
    for m in range(4):
        stat_send[1, m] = jnp.sum(sm[m], axis=0, keepdims=True)
    for p in (2, 3, 1):
        start(rcopy(stat_send, stat_recv.at[p], st_ssem.at[p], st_rsem.at[p], mate(p)))
    turn(1, 2)
    shared(1, 1)
    turn(1, 1)
    shared(1, 3)
    turn(1, 3)
    for p in (1, 2, 3):
        rcopy(stat_send, stat_recv.at[p], st_ssem.at[p], st_rsem.at[p], mate(p)).wait_recv()
    for m in range(4):
        tops = [stat_send[0, m]] + [stat_recv[p, 0, m ^ p] for p in (1, 2, 3)]
        sums = [stat_send[1, m]] + [stat_recv[p, 1, m ^ p] for p in (1, 2, 3)]
        top = functools.reduce(jnp.maximum, tops)
        parts = [jnp.exp(v - top) for v in tops]
        total = sum(u * v for u, v in zip(parts, sums))
        sm[m] = jnp.broadcast_to(parts[0] / total, (8, rows))

    def to_y(a, k, value):
        if k:
            y_send[a, k] = value.astype(BF16)
            start(rcopy(y_send.at[a, k], y_recv.at[a, k], fy_send.at[a, k], fy_recv.at[a, k], yline(k)))
        else:
            acc[a] = value

    p = by_row(st_r[...], sm[0], jnp.multiply).astype(BF16)
    pb_r[...] = p
    for k in (3, 2, 1, 0):
        b = flip(y, k)
        for m in range(4):
            pb[b, :, m * rows : (m + 1) * rows] = by_row(st[b, m], sm[m], jnp.multiply).astype(BF16)
        to_y(1, k, jnp.dot(pb[b], qd[1].reshape(4 * rows, HD), preferred_element_type=F32))
    rg_acc[1] = jnp.dot(p, qd[1, 0], preferred_element_type=F32)

    d = jnp.dot(rkv[1], qd_t[1, 0], preferred_element_type=F32)
    dp_r[...] = d
    dl[0] = fold(pb_r[...].astype(F32) * d, jnp.sum)
    for m in range(1, 4):
        dl[m] = jnp.zeros((8, rows), F32)
    for v in classes:
        b = arrived(1, v)
        for m in range(4):
            d = jnp.dot(kv[1, b], qd_t[1, m], preferred_element_type=F32)
            dp[b, m] = d
            dl[m] += fold(pb[b, :, m * rows : (m + 1) * rows].astype(F32) * d, jnp.sum)
    for m in range(4):
        del_send[m] = jnp.sum(dl[m], axis=0, keepdims=True)
    for p in (2, 3, 1):
        start(rcopy(del_send, del_recv.at[p], de_ssem.at[p], de_rsem.at[p], mate(p)))

    def sum_y(a):
        total = acc[a]
        for k in (1, 3, 2):
            rcopy(y_send.at[a, k], y_recv.at[a, k], fy_send.at[a, k], fy_recv.at[a, k], yline(k)).wait_recv()
            total = total + y_recv[a, k].astype(F32)
        p_send[a] = total.astype(BF16).reshape(2, 4 * TILE, HD)
        for k in range(2):
            home = rcopy(p_send.at[a, k], p_recv.at[a, h], fp_send.at[a, k], fp_recv.at[a, h], owner(k))
            local = pltpu.make_async_copy(p_send.at[a, k], p_recv.at[a, h], fp_recv.at[a, h])
            pl.when(jnp.logical_not(own(k)))(home.start)
            pl.when(own(k))(local.start)

    for p in (1, 2, 3):
        rcopy(del_send, del_recv.at[p], de_ssem.at[p], de_rsem.at[p], mate(p)).wait_recv()
    for m in range(4):
        total = del_send[m] + del_recv[1, m ^ 1] + del_recv[2, m ^ 2] + del_recv[3, m ^ 3]
        dl[m] = jnp.broadcast_to(total, (8, rows))

    def d_score(e, d, m):
        return (by_row(e, sm[m], jnp.multiply) * by_row(d, dl[m], jnp.subtract)).astype(BF16)

    for k in (3, 2, 1, 0):
        b = flip(y, k)
        for m in range(4):
            pb[b, :, m * rows : (m + 1) * rows] = d_score(st[b, m], dp[b, m], m)
        to_y(0, k, jnp.dot(pb[b], qd[0].reshape(4 * rows, HD), preferred_element_type=F32) * scale)
    ds = d_score(st_r[...], dp_r[...], 0)
    pb_r[...] = ds
    rg_acc[0] = jnp.dot(ds, qd[0, 0], preferred_element_type=F32) * scale
    own_rows = count // n_tp
    rg = jnp.concatenate(
        [rg_acc[0].reshape(n_tp, own_rows, HD), rg_acc[1].reshape(n_tp, own_rows, HD)], axis=1
    )
    rg_send[...] = rg.astype(BF16)

    def spread(d, carry):
        to = lax.rem(t + d, n_tp)
        rcopy(rg_send.at[to], rg_recv.at[t], rg_ssem.at[0], rg_rsem.at[0], {"resp": r, "tp": to}).start()
        return carry

    lax.fori_loop(1, n_tp, spread, 0)
    pltpu.make_async_copy(rg_send.at[t], rg_recv.at[t], rg_rsem.at[0]).start()

    def tdot(a, b):
        return lax.dot_general(a, b, (((0,), (0,)), ((), ())), preferred_element_type=F32)

    keys = kv[0].reshape(n_y * 8 * TILE, HD)

    def dq_part(m):
        return tdot(keys, pb[:, :, m * rows : (m + 1) * rows].reshape(n_y * 8 * TILE, rows))

    dqs_send[0] = dq_part(1).astype(BF16)
    dqs_send[1] = dq_part(3).astype(BF16)
    start(rcopy(dqs_send, dqs_recv, dq_ssem.at[0], dq_rsem.at[0], mate(1)))
    there = dq_part(2)
    rcopy(dqs_send, dqs_recv, dq_ssem.at[0], dq_rsem.at[0], mate(1)).wait_recv()
    dqz_send[...] = (there + dqs_recv[1].astype(F32)).astype(BF16)
    start(rcopy(dqz_send, dqz_recv, dq_ssem.at[1], dq_rsem.at[1], mate(2)))
    sum_y(1)
    dq_t = dq_part(0) + tdot(rkv[0], pb_r[...]) + dqs_recv[0].astype(F32)
    sum_y(0)
    rcopy(dqz_send, dqz_recv, dq_ssem.at[1], dq_rsem.at[1], mate(2)).wait_recv()
    dq_t = dq_t + dqz_recv[...].astype(F32)
    for j in range(heads):
        dq_ref[:, j * HD : (j + 1) * HD] = jnp.transpose(dq_t[:, j * count : (j + 1) * count]) * scale

    pltpu.make_async_copy(rg_recv, rg_recv, rg_rsem.at[0]).wait()
    got = rg_recv[...].astype(F32)
    for i in range(n_tp // 2):
        both = got[2 * i] + got[2 * i + 1]
        rdk_ref[:, i * HD : (i + 1) * HD] = both[:own_rows]
        rdv_ref[:, i * HD : (i + 1) * HD] = both[own_rows:]

    first = 2 * lax.rem(r, n_z // 2)
    for a, ref in ((1, pdv_ref), (0, pdk_ref)):
        for i in range(2):
            got = p_recv.at[a, i]
            rcopy(got, got, fp_send.at[a, i], fp_recv.at[a, i], mate(1)).wait_recv()
            for d in range(4):
                at = lax.rem(first + n_z - d, n_z) if i == 0 else lax.rem(first + 1 + d, n_z)
                ref[pl.ds(pl.multiple_of(at * TILE, TILE), TILE)] = got[d * TILE : (d + 1) * TILE].astype(F32)

    for a in range(2):
        out = sent.at[pl.ds(0, len(offsets))]
        pltpu.make_async_copy(out, out, a_send.at[a]).wait()
    out = rg_send.at[pl.ds(0, n_tp - 1)]
    pltpu.make_async_copy(out, out, rg_ssem.at[0]).wait()
    for copy in sends:
        copy.wait_send()
    for a in range(2):
        for k in range(2):
            home = rcopy(p_send.at[a, k], p_recv.at[a, h], fp_send.at[a, k], fp_recv.at[a, h], owner(k))
            pl.when(jnp.logical_not(own(k)))(home.wait_send)


def write_out(*refs):
    sem = refs[10]
    copies = [pltpu.make_async_copy(refs[i], refs[5 + i], sem.at[i]) for i in range(5)]
    for copy in copies:
        copy.start()
    for copy in copies:
        copy.wait()


def solution(mesh):
    n_resp, n_tp = mesh.shape["resp"], mesh.shape["tp"]
    n_y = n_resp // 2

    def per_device(queries, resp_keys, resp_values, prefix_keys, prefix_values, cotangent, lengths):
        count, width = queries.shape
        heads = width // HD
        rows = heads * count
        half = n_tp // 2 * TILE
        cols = prefix_keys.shape[1]
        dma = pltpu.SemaphoreType.DMA
        vmem = pltpu.VMEM
        any_spec = pl.BlockSpec(memory_space=pl.ANY)
        vmem_spec = pl.BlockSpec(memory_space=pltpu.VMEM)
        shapes = ((count, width), (count // n_tp, cols), (count // n_tp, cols), (half, HD), (half, HD))
        results = pl.pallas_call(
            functools.partial(kernel, n_resp, n_tp),
            out_shape=tuple(pltpu.VMEM(shape, F32) for shape in shapes),
            in_specs=[any_spec] * 6 + [pl.BlockSpec(memory_space=pltpu.SMEM)],
            out_specs=(vmem_spec,) * 5,
            scratch_shapes=[
                vmem((2, TILE, cols), BF16),
                vmem((2, n_y, half, HD), BF16),
                vmem((2, count, HD), BF16),
                vmem((2, 4, rows, HD), BF16),
                vmem((2, 4, HD, rows), BF16),
                vmem((n_y, 4, half, rows), F32),
                vmem((n_y, 4, half, rows), F32),
                vmem((n_y, half, 4 * rows), BF16),
                vmem((count, rows), F32),
                vmem((count, rows), F32),
                vmem((count, rows), BF16),
                vmem((4, 8, rows), F32),
                vmem((4, 8, rows), F32),
                vmem((4, 8, rows), F32),
                vmem((2, 4, 1, rows), F32),
                vmem((4, 2, 4, 1, rows), F32),
                vmem((4, 1, rows), F32),
                vmem((4, 4, 1, rows), F32),
                vmem((2, half, HD), F32),
                vmem((2, n_y, half, HD), BF16),
                vmem((2, n_y, half, HD), BF16),
                vmem((2, 2, half // 2, HD), BF16),
                vmem((2, 2, half // 2, HD), BF16),
                vmem((n_tp, 16, HD), BF16),
                vmem((n_tp, 16, HD), BF16),
                vmem((2, count, HD), F32),
                vmem((2, HD, rows), BF16),
                vmem((2, HD, rows), BF16),
                vmem((HD, rows), BF16),
                vmem((HD, rows), BF16),
                vmem((n_resp * 4, TILE, HD), BF16),
                dma((4 + 2 * heads,)),
                dma((2,)),
                dma((2, n_y)),
                dma((2, 4)),
                dma((2, 4)),
                dma((4,)),
                dma((4,)),
                dma((4,)),
                dma((4,)),
                dma((2, n_y)),
                dma((2, n_y)),
                dma((2, 2)),
                dma((2, 2)),
                dma((1,)),
                dma((1,)),
                dma((2,)),
                dma((2,)),
            ],
            compiler_params=pltpu.CompilerParams(
                collective_id=0, has_side_effects=True, vmem_limit_bytes=62 * 1024 * 1024
            ),
            cost_estimate=pl.CostEstimate(
                flops=10 * rows * (n_resp * 2 * half + count) * HD,
                bytes_accessed=4 * 1024 * 1024,
                transcendentals=rows * (n_resp * 2 * half + count),
            ),
        )(queries, resp_keys, resp_values, prefix_keys, prefix_values, cotangent, lengths)
        return pl.pallas_call(
            write_out,
            out_shape=tuple(jax.ShapeDtypeStruct(shape, F32) for shape in shapes),
            in_specs=[any_spec] * 5,
            out_specs=(any_spec,) * 5,
            scratch_shapes=[dma((5,))],
            compiler_params=pltpu.CompilerParams(vmem_limit_bytes=256 * 1024),
        )(*results)

    return jax.shard_map(
        per_device,
        mesh=mesh,
        in_specs=(
            P(("grp", "resp"), "tp"),
            P(("grp", "resp"), None),
            P(("grp", "resp"), None),
            P(("grp", "resp", "tp"), None),
            P(("grp", "resp", "tp"), None),
            P(("grp", "resp"), "tp"),
            P("grp"),
        ),
        out_specs=(
            P(("grp", "resp"), "tp"),
            P(("grp", "resp", "tp"), None),
            P(("grp", "resp", "tp"), None),
            P(("grp", "tp"), "resp"),
            P(("grp", "tp"), "resp"),
        ),
        check_vma=False,
    )
```
